512 devices in a mesh: learn: 16 (over z, core), ep: 32 (over x, y).
Axes of the slice: x: 4, y: 8, z: 8, core: 2. Of those that a mesh axis runs over, the one named last changes fastest.
Arguments:
- master_weight: float32 [7168, 3, 32, 256], P(('learn', 'ep')), may hold values from -0.125 to 0.125
- gradient: bfloat16 [7168, 3, 32, 256], P(('learn', 'ep')), may hold values from -6 to 6
- first_moment: bfloat16 [7168, 3, 32, 256], P(('learn', 'ep')), may hold values from -1.5 to 1.5
- second_moment: bfloat16 [7168, 3, 32, 256], P(('learn', 'ep')), may hold values from 0.0099487305 to 0.29882812
- block_slot: int32 [32], replicated, may hold values from 0 to 31, each once
- queries: bfloat16 [2, 512, 32, 576], P(None, 'ep', 'learn'), may hold values from -512 to 512
- kv_cache: bfloat16 [512, 24, 576], P('ep'), may hold values from -512 to 512
- new_latent: bfloat16 [2, 512, 576], P(None, 'ep'), may hold values from -512 to 512
- lengths: int32 [512], P('ep'), may hold values from 1 to 24, 6144 in all
- uv_weight: bfloat16 [32, 512, 128], P('learn'), may hold values from -1 to 1
- out_weight: bfloat16 [32, 128, 7168], P('learn', None, 'ep'), may hold values from -0.09375 to 0.09375
- residual: bfloat16 [2, 512, 7168], P(None, ('learn', 'ep')), may hold values from -6 to 6
- norm_gain: float32 [7168], replicated, may hold values from 0.1 to 1.9
- expert_ids: int32 [2, 512, 8], P(None, ('learn', 'ep')), may hold values from 0 to 191, as said below
- route_weight: float32 [2, 512, 8], P(None, ('learn', 'ep')), may hold values from 0.05 to 1
Outputs:
- layer_out: bfloat16 [2, 512, 7168], P(None, ('learn', 'ep'))
The draws below stay inside these ranges and needn't reach their ends.
Inputs may be any that keep to these rules, and one draw needn't show every extreme that they name: `block_slot`: each learner block is named once. `expert_ids`: each row names 8 different experts, two to four of them below 8.
All inputs are finite; a program needn't handle non-finite values. No bound on the sum of `lengths` on one device may be relied on, other than what follows from the above.
Results may differ from the reference program's by a relative error of at most 0.012.
Values may be sent and summed in bfloat16 or wider, within the bound.
A program may use at most 128 MiB of HBM per device.

```python
import math
import jax
import jax.numpy as jnp
import numpy as np
from jax import lax

D = 7168
LAT = 512
ROPE = 64
VH = 128
NH = 32
HID = 1024
BH = 256
BPE = 4
EXPERTS = 8
NEXP = 192
TOPK = 8
BLOCKS = 32
CACHE = 24
STEPS = 2
ROWS = 512


def attention_parts(key):
    width = LAT + ROPE
    cache_part = jnp.clip(jax.random.normal(jax.random.fold_in(key, 101), (ROWS, CACHE, width), jnp.float32), -6.0, 6.0)
    fresh_part = jnp.clip(jax.random.normal(jax.random.fold_in(key, 102), (STEPS, ROWS, width), jnp.float32), -6.0, 6.0)
    query_part = jnp.clip(jax.random.normal(jax.random.fold_in(key, 103), (STEPS, ROWS, NH, width), jnp.float32), -6.0, 6.0)
    return (cache_part, fresh_part, query_part)


def draw_queries(key, part):
    cache_part, fresh_part, query_part = attention_parts(key)
    return query_part.astype(jnp.bfloat16)


def draw_kv_cache(key, part):
    cache_part, fresh_part, query_part = attention_parts(key)
    return cache_part.astype(jnp.bfloat16)


def draw_new_latent(key, part):
    cache_part, fresh_part, query_part = attention_parts(key)
    return fresh_part.astype(jnp.bfloat16)


def draw_expert_ids(key, part):
    key = jax.random.fold_in(key, 7)
    window_count = jax.random.randint(jax.random.fold_in(key, 1), (STEPS, ROWS), 2, 5)
    window_score = jax.random.randint(jax.random.fold_in(key, 2), (STEPS, ROWS, EXPERTS), 0, 2 ** 20) * EXPERTS + jnp.arange(EXPERTS)
    window_order = jnp.argsort(-window_score, axis=2).astype(jnp.int32)
    other_total = NEXP - EXPERTS
    other_score = jax.random.randint(jax.random.fold_in(key, 3), (STEPS, ROWS, other_total), 0, 2 ** 20) * other_total + jnp.arange(other_total)
    other_values, other_order = jax.lax.top_k(other_score, TOPK)
    other_ids = other_order.astype(jnp.int32) + EXPERTS
    slot_index = jnp.arange(TOPK)
    window_pick = jnp.take_along_axis(window_order, jnp.broadcast_to(jnp.minimum(slot_index, EXPERTS - 1), (STEPS, ROWS, TOPK)), axis=2)
    other_slot = jnp.clip(slot_index[None, None, :] - window_count[:, :, None], 0, TOPK - 1)
    other_pick = jnp.take_along_axis(other_ids, other_slot, axis=2)
    return jnp.where(slot_index[None, None, :] < window_count[:, :, None], window_pick, other_pick).astype(jnp.int32)


def block_scale(stream_key, extent, cuts, least, largest):
    def one(dim, parts):
        draws = jax.random.uniform(jax.random.fold_in(jax.random.fold_in(stream_key, 6), dim), (parts,), jnp.float32, least / len(cuts), largest / len(cuts))
        return jnp.repeat(jnp.exp(draws), extent[dim] // parts).reshape((-1,) + (1,) * (len(extent) - dim - 1))

    factor_of = one(*cuts[0])
    for cut in cuts[1:]:
        factor_of = factor_of * one(*cut)
    return factor_of


def split_up(number_of, total, limit, lean):
    portions = [(1 << 20) // math.isqrt(rank ** lean) + 1 for rank in range(2, number_of + 1)]
    surplus, counts = total - limit - (number_of - 1), [1] * (number_of - 1)
    while surplus > 0:
        movable = [i for i in range(number_of - 1) if counts[i] < limit]
        mass, budget = sum([portions[i] for i in movable]), surplus
        for i in movable:
            addition = min(limit - counts[i], max(1, budget * portions[i] // mass), surplus)
            counts[i] = counts[i] + addition
            surplus = surplus - addition
    return np.array([limit] + counts)


def ragged_sizes(rng, count, total, bound, slope):
    if count == 2:
        one = jax.random.randint(rng, (), max(1, total - bound), min(bound, total - 1) + 1)
        return jnp.stack([one, total - one])
    tallies = jnp.asarray(split_up(count, total, bound, slope), jnp.int32)
    pairs = (count - 1) // 2
    donor, sink = tallies[1:1 + 2 * pairs:2], tallies[2:2 + 2 * pairs:2]
    margin = jnp.minimum(donor - 1, bound - sink)
    shifted = jax.random.randint(jax.random.fold_in(rng, 1), (pairs,), 0, 1 << 20) % (margin + 1)
    tallies = tallies.at[1:1 + 2 * pairs:2].set(donor - shifted).at[2:2 + 2 * pairs:2].set(sink + shifted)
    return tallies[jax.random.permutation(jax.random.fold_in(rng, 2), count)]


def normal_values(key, dims, scale, bound, shards=(), held_as=jnp.bfloat16):
    array = scale * jax.random.normal(key, dims, jnp.float32)
    if shards:
        array = array * block_scale(key, dims, shards, -0.22, 0.18)
    return jnp.clip(array, -bound, bound).astype(held_as)


def setup_inputs(seed: int = 0) -> dict:
    seeds = jax.random.split(jax.random.key(seed), 16)
    master_weight = normal_values(seeds[0], (D, 3, BLOCKS, BH), (2 * HID) ** -0.5, 0.125, ((0, 512),), jnp.float32)
    gradient = normal_values(seeds[1], (D, 3, BLOCKS, BH), 1.0, 6.0, ((0, 512),))
    first_moment = normal_values(seeds[2], (D, 3, BLOCKS, BH), 0.1, 1.5, ((0, 512),))
    second_moment = jnp.clip(jnp.exp(math.log(0.29882812) - 3.4024236 * jax.random.uniform(seeds[3], (D, 3, BLOCKS, BH), jnp.float32) ** block_scale(seeds[3], (D, 3, BLOCKS, BH), ((0, 512),), -0.2, 0.2)), 0.0099487305, 0.29882812).astype(jnp.bfloat16)
    block_slot = jax.random.permutation(seeds[4], BLOCKS).astype(jnp.int32)
    queries = draw_queries(jax.random.fold_in(seeds[15], 71), 0)
    kv_cache = draw_kv_cache(jax.random.fold_in(seeds[15], 71), 0)
    new_latent = draw_new_latent(jax.random.fold_in(seeds[15], 71), 0)
    lengths = ragged_sizes(seeds[8], ROWS, ROWS * CACHE // 2, CACHE, 2).astype(jnp.int32)
    uv_weight = normal_values(seeds[9], (NH, LAT, VH), (LAT // 16) ** -0.5, 1.0, ((0, 16),))
    out_weight = normal_values(seeds[10], (NH, VH, D), (NH * VH) ** -0.5, 0.09375, ((0, 16), (2, 32)))
    residual = normal_values(seeds[11], (STEPS, ROWS, D), 0.5, 6.0, ((1, 512),))
    norm_gain = jnp.clip(1.0 + 0.18 * jax.random.normal(seeds[12], (D,), jnp.float32), 0.1, 1.9)
    expert_ids = draw_expert_ids(jax.random.fold_in(seeds[15], 71), 0)
    route_weight = jnp.clip(jnp.exp(math.log(1.0) - 2.9957323 * jax.random.uniform(seeds[14], (STEPS, ROWS, TOPK), jnp.float32) ** block_scale(seeds[14], (STEPS, ROWS, TOPK), ((1, 512),), -0.2, 0.2)), 0.05, 1.0)
    return dict(master_weight=master_weight, gradient=gradient, first_moment=first_moment, second_moment=second_moment, block_slot=block_slot, queries=queries, kv_cache=kv_cache, new_latent=new_latent, lengths=lengths, uv_weight=uv_weight, out_weight=out_weight, residual=residual, norm_gain=norm_gain, expert_ids=expert_ids, route_weight=route_weight)


beta_one = 0.9
beta_two = 0.95
learn_rate = 0.01
adam_step = 50
adam_epsilon = 1e-08
norm_epsilon = 1e-06
route_scale = 2.827

def adam_update(master_weight, gradient, first_moment, second_moment):
    grad_value = gradient.astype(jnp.float32)
    first_new = beta_one * first_moment.astype(jnp.float32) + (1.0 - beta_one) * grad_value
    second_new = beta_two * second_moment.astype(jnp.float32) + (1.0 - beta_two) * grad_value * grad_value
    first_fix = 1.0 - beta_one ** adam_step
    second_fix = 1.0 - beta_two ** adam_step
    stride = first_new / first_fix / (jnp.sqrt(second_new / second_fix) + adam_epsilon)
    return (master_weight - learn_rate * stride).astype(jnp.bfloat16)

def invert_slot(block_slot):
    slot_count = block_slot.shape[0]
    order_ids = jnp.arange(slot_count).astype(jnp.int32)
    match_table = (block_slot[None, :] == order_ids[:, None]).astype(jnp.int32)
    return lax.optimization_barrier(jnp.sum(match_table * order_ids[None, :], axis=1)).astype(jnp.int32)

def attend_heads(query_rows, cache_rows, new_keys, lengths, uv_weight):
    key_rows = jnp.concatenate([cache_rows, new_keys], axis=1)
    key_count = key_rows.shape[1]
    position = jnp.arange(key_count).astype(jnp.int32)
    live_mask = (position[None, :] < lengths[:, None]) | (position[None, :] >= cache_rows.shape[1])
    scores = jnp.einsum('rhk,rck->rhc', query_rows.astype(jnp.float32), key_rows.astype(jnp.float32))
    scores = scores * (VH + ROPE) ** (-0.5)
    scores = jnp.where(live_mask[:, None, :], scores, -1e+30)
    row_max = lax.optimization_barrier(jnp.max(scores, axis=2, keepdims=True))
    raised = jnp.exp(scores - row_max)
    soft_weight = (raised / lax.optimization_barrier(jnp.sum(raised, axis=2, keepdims=True))).astype(jnp.bfloat16)
    latent = jnp.einsum('rhc,rcl->rhl', soft_weight.astype(jnp.float32), key_rows[:, :, :LAT].astype(jnp.float32)).astype(jnp.bfloat16)
    heads_out = jnp.einsum('rhl,hlv->rhv', latent.astype(jnp.float32), uv_weight.astype(jnp.float32)).astype(jnp.bfloat16)
    return heads_out

def scale_norm(hidden_state, norm_gain):
    spread_sq = lax.optimization_barrier(jnp.mean(hidden_state * hidden_state, axis=-1, keepdims=True))
    return (hidden_state * lax.rsqrt(spread_sq + norm_epsilon) * norm_gain.astype(jnp.float32)).astype(jnp.bfloat16)

def block_shares(expert_ids, route_weight):
    route_value = route_weight.astype(jnp.float32)
    route_share = route_value / lax.optimization_barrier(jnp.sum(route_value, axis=1, keepdims=True)) * route_scale
    expert_index = jnp.arange(EXPERTS).astype(jnp.int32)
    hit_table = (expert_ids[:, :, None] == expert_index[None, None, :]).astype(jnp.float32)
    per_expert = lax.optimization_barrier(jnp.sum(route_share[:, :, None] * hit_table, axis=1))
    return jnp.repeat(per_expert, BPE, axis=1)

def experts_sum(normed, expert_weights, block_share):

    def one_block(running, block_index):
        weights = lax.dynamic_index_in_dim(expert_weights, block_index, 2, keepdims=False)
        gate_value = jnp.dot(normed, weights[:, 0, :], preferred_element_type=jnp.float32)
        up_value = jnp.dot(normed, weights[:, 1, :], preferred_element_type=jnp.float32)
        activation = (jax.nn.silu(gate_value) * up_value).astype(jnp.bfloat16)
        block_out = lax.dot_general(activation, weights[:, 2, :], (((1,), (1,)), ((), ())), preferred_element_type=jnp.float32).astype(jnp.bfloat16)
        weight_col = lax.dynamic_index_in_dim(block_share, block_index, 1, keepdims=False)
        return (running + weight_col[:, None] * block_out.astype(jnp.float32), None)
    start_sum = jnp.zeros((normed.shape[0], normed.shape[1]), jnp.float32)
    running, unused = lax.scan(one_block, start_sum, jnp.arange(BLOCKS).astype(jnp.int32))
    return running

def reference(master_weight, gradient, first_moment, second_moment, block_slot, queries, kv_cache, new_latent, lengths, uv_weight, out_weight, residual, norm_gain, expert_ids, route_weight):
    updated = adam_update(master_weight, gradient, first_moment, second_moment)
    expert_weights = jnp.take(updated, invert_slot(block_slot), axis=2)
    out_flat = out_weight.reshape(NH * VH, D)
    results = []
    for decode_step in range(STEPS):
        new_keys = jnp.transpose(new_latent[:decode_step + 1], (1, 0, 2))
        heads_out = attend_heads(queries[decode_step], kv_cache, new_keys, lengths, uv_weight)
        attended = jnp.dot(heads_out.reshape(ROWS, NH * VH), out_flat, preferred_element_type=jnp.float32).astype(jnp.bfloat16)
        hidden_state = residual[decode_step].astype(jnp.float32) + attended.astype(jnp.float32)
        normed = scale_norm(hidden_state, norm_gain)
        block_share = block_shares(expert_ids[decode_step], route_weight[decode_step])
        routed = experts_sum(normed, expert_weights, block_share)
        results.append((hidden_state + routed).astype(jnp.bfloat16))
    return jnp.stack(results)
```

```python
import functools

import jax
import jax.numpy as jnp
from jax import lax
from jax.experimental import pallas as pl
from jax.experimental.pallas import tpu as pltpu
from jax.sharding import PartitionSpec as P

BF = jnp.bfloat16
F32 = jnp.float32
MESH = pl.DeviceIdType.MESH

beta_one = 0.9
beta_two = 0.95
learn_rate = 0.01
adam_step = 50
adam_epsilon = 1e-08
norm_epsilon = 1e-06
route_scale = 2.827

NX, NY, NZ, NL, NE = 4, 8, 8, 16, 32
WIDTH, SLICE, PART = 7168, 448, 224
LANES = 512
SS_LANE, SHARE_HI, SHARE_LO = 448, 456, 464
EXPERTS, STEPS, CACHE, LAT = 8, 2, 24, 512


def dot(a, b):
    return jnp.dot(a, b, preferred_element_type=F32)


def dot_t(a, b):
    return lax.dot_general(a, b, (((1,), (1,)), ((), ())), preferred_element_type=F32)


def iota(shape, dim):
    return lax.broadcasted_iota(jnp.int32, shape, dim)


def adam_kernel(slot_ref, mw_ref, gr_ref, fm_ref, sm_ref, out_ref, rows_ref):
    d = pl.program_id(0)

    @pl.when(d == 0)
    def _():
        rows_ref[...] = jnp.zeros_like(rows_ref)

    order = (slot_ref[...] == iota((NE, NE), 0)).astype(BF)
    first_fix = 1.0 - beta_one**adam_step
    second_fix = 1.0 - beta_two**adam_step
    for m in range(3):
        g = gr_ref[0, m].astype(F32)
        first_new = beta_one * fm_ref[0, m].astype(F32) + (1.0 - beta_one) * g
        second_new = beta_two * sm_ref[0, m].astype(F32) + (1.0 - beta_two) * g * g
        stride = first_new / first_fix / (jnp.sqrt(second_new / second_fix) + adam_epsilon)
        updated = (mw_ref[0, m] - learn_rate * stride).astype(BF)
        ordered = dot(order, updated)
        rows_ref[0, pl.ds(m * 16 + d, NE, stride=48), :] = ordered[:, :128]
        rows_ref[1, pl.ds(m * 16 + d, NE, stride=48), :] = ordered[:, 128:]

    @pl.when(d == pl.num_programs(0) - 1)
    def _():
        for half in range(2):
            out_ref[:, :, 128 * half : 128 * half + 128] = (
                rows_ref[half].reshape(NE, 48, 128).astype(BF)
            )


def adam_blocks(master_weight, gradient, first_moment, second_moment, block_slot):
    depth = master_weight.shape[0]
    spec = pl.BlockSpec((1, 3, NE, 256), lambda d: (d, 0, 0, 0))
    return pl.pallas_call(
        adam_kernel,
        grid=(depth,),
        out_shape=jax.ShapeDtypeStruct((NE, 48, 256), BF),
        in_specs=[pl.BlockSpec((1, NE), lambda d: (0, 0)), spec, spec, spec, spec],
        out_specs=pl.BlockSpec((NE, 48, 256), lambda d: (0, 0, 0)),
        scratch_shapes=[pltpu.VMEM((2, NE * 48, 128), F32)],
        compiler_params=pltpu.CompilerParams(vmem_limit_bytes=32 * 2**20),
        name="adam_blocks",
    )(block_slot.reshape(1, NE), master_weight, gradient, first_moment, second_moment)


def wait_bytes(ref, sem):
    pltpu.make_async_copy(ref, ref, sem).wait()


def remote(src, dst, ssem, rsem, device):
    return pltpu.make_async_remote_copy(
        src_ref=src, dst_ref=dst, send_sem=ssem, recv_sem=rsem, device_id=device, device_id_type=MESH
    )


def layer_kernel(
    q_ref, kk_ref, len_ref, uv_ref, ow_ref, res_ref, gain_ref, ws_ref, out_ref,
    heads, att_s, att_r, mov_s, mov_r, res_r, hid, rows, w_r, w_n,
    gate_s, gate_o, gate_r, sum_s, sum_r, sq_s, sq_r, sq_t, sq_z, acts, down_s, down_r,
    y_s, y_r, fin_s, fin_r, share,
    s_sem, r_sem, hy_sem, xy_sem,
):
    l = lax.axis_index("learn")
    e = lax.axis_index("ep")
    x, y = e // NY, lax.rem(e, NY)
    z, c = l // 2, lax.rem(l, 2)
    sib = {"learn": l + 1 - 2 * c}

    barrier = pltpu.get_barrier_semaphore()

    def greet_ep(k, carry):
        pl.semaphore_signal(barrier, inc=1, device_id={"ep": lax.rem(e + k, NE)}, device_id_type=MESH)
        return carry

    def greet_learn(k, carry):
        pl.semaphore_signal(barrier, inc=1, device_id={"learn": lax.rem(l + k, NL)}, device_id_type=MESH)
        return carry

    lax.fori_loop(1, NE, greet_ep, 0)
    lax.fori_loop(1, NL, greet_learn, 0)
    own_move = e // 2 == l
    for j in range(2):
        @pl.when(jnp.logical_not(jnp.logical_and(own_move, lax.rem(e, 2) == j)))
        def _():
            pl.semaphore_signal(
                barrier, inc=1, device_id={"learn": e // 2, "ep": 2 * l + j}, device_id_type=MESH
            )
    pl.semaphore_wait(barrier, NE - 1 + NL - 1 + 2 - own_move.astype(jnp.int32))

    res_r[l] = res_ref[l]

    def send_res(k, carry):
        t = lax.rem(l + k, NL)
        remote(res_ref.at[t], res_r.at[l], s_sem.at[0], r_sem.at[0], {"learn": t}).start()
        return carry

    lax.fori_loop(1, NL, send_res, 0)

    keys = kk_ref[...]
    scores = dot_t(q_ref[...], keys) * (192.0 ** (-0.5))
    shape = scores.shape
    row, col = iota(shape, 0), iota(shape, 1)
    row_i = lax.rem(row, 16)
    cached = 16 * CACHE
    first = row_i * CACHE
    live = jnp.logical_and(col >= first, col < first + len_ref[...])
    live = jnp.logical_or(live, col == cached + row_i)
    live = jnp.logical_or(live, jnp.logical_and(col == cached + 16 + row_i, row >= 32))
    scores = jnp.where(live, scores, -1e30)
    raised = jnp.exp(scores - jnp.max(scores, axis=1, keepdims=True))
    soft = (raised / jnp.sum(raised, axis=1, keepdims=True)).astype(BF)
    latent = dot(soft, keys[:, :LAT]).astype(BF)
    for s in range(STEPS):
        for h in range(2):
            start = s * 32 + h * 16
            heads[s, e, :, 128 * h : 128 * h + 128] = dot(
                latent[start : start + 16], uv_ref[h]
            ).astype(BF)

    def gather_start(buf, i, ysem, xsem):
        def send_y(k, carry):
            t = x * NY + lax.rem(y + k, NY)
            remote(buf.at[e], buf.at[e], s_sem.at[i], ysem.at[k], {"ep": t}).start()
            return carry

        def send_x(k, carry):
            t = lax.rem(x + k, NX) * NY + y
            remote(buf.at[e], buf.at[e], s_sem.at[i], xsem, {"ep": t}).start()
            return carry

        lax.fori_loop(1, NY, send_y, 0)
        lax.fori_loop(1, NX, send_x, 0)

    def gather_finish(buf, i, ysem, xsem):
        def relay(t, carry):
            half = t // 2
            k = jnp.where(lax.rem(t, 2) == 0, half + 1, NY - 1 - half)
            o = x * NY + lax.rem(y + NY - k, NY)
            wait_bytes(buf.at[o], ysem.at[k])

            def send_x(j, carry2):
                d = lax.rem(x + j, NX) * NY + y
                remote(buf.at[o], buf.at[o], s_sem.at[i], xsem, {"ep": d}).start()
                return carry2

            return lax.fori_loop(1, NX, send_x, carry)

        lax.fori_loop(0, NY - 1, relay, 0)
        wait_bytes(buf.at[pl.ds(0, NE - NY)], xsem)

    for s in range(STEPS):
        gather_start(heads.at[s], 1 + s, hy_sem.at[s], r_sem.at[1 + s])

    w_r[e] = ws_ref[e]

    def send_w(k, carry):
        t = lax.rem(e + k, NE)
        remote(ws_ref.at[t], w_r.at[e], s_sem.at[3], r_sem.at[3], {"ep": t}).start()
        return carry

    tokens = 512
    n, m = iota((tokens, tokens), 0), iota((tokens, tokens), 1)
    reorder = (m == 32 * lax.rem(n, 16) + n // 16).astype(BF)
    for s in range(STEPS):
        gather_finish(heads.at[s], 1 + s, hy_sem.at[s], r_sem.at[1 + s])
        ordered = dot(reorder, heads[s].reshape(tokens, 256)).astype(BF)
        att_s[s] = dot(ordered, ow_ref[...]).astype(BF).reshape(NL, 32, 256)
        att_r[s, l] = att_s[s, l]

        def send_att(k, carry):
            t = lax.rem(l + k, NL)
            remote(att_s.at[s, t], att_r.at[s, l], s_sem.at[4 + s], r_sem.at[4 + s], {"learn": t}).start()
            return carry

        lax.fori_loop(1, NL, send_att, 0)

    lax.fori_loop(1, NE, send_w, 0)

    for s in range(STEPS):
        wait_bytes(att_r.at[s, pl.ds(0, NL - 1)], r_sem.at[4 + s])
        total = att_r[s, 0].astype(F32)
        for k in range(1, NL):
            total = total + att_r[s, k].astype(F32)
        mov_s[s] = total.astype(BF).reshape(2, 16, 256)
        for j in range(2):
            here = jnp.logical_and(own_move, lax.rem(e, 2) == j)

            @pl.when(here)
            def _():
                mov_r[s, lax.rem(e, 2)] = mov_s[s, j]

            @pl.when(jnp.logical_not(here))
            def _():
                remote(
                    mov_s.at[s, j], mov_r.at[s, lax.rem(e, 2)], s_sem.at[6 + s], r_sem.at[6 + s],
                    {"learn": e // 2, "ep": 2 * l + j},
                ).start()

    def move_wait(s, sem):
        @pl.when(own_move)
        def _():
            wait_bytes(mov_r.at[s, 0], sem)

        @pl.when(jnp.logical_not(own_move))
        def _():
            wait_bytes(mov_r.at[s], sem)

    wait_bytes(res_r.at[pl.ds(0, NL - 1)], r_sem.at[0])
    lane = iota((16, LANES), 1)
    spread_row, spread_col = iota((256, LANES), 0), iota((256, LANES), 1)
    real = spread_row < PART
    place0 = jnp.logical_and(real, spread_col == spread_row).astype(BF)
    place1 = jnp.logical_and(real, spread_col == spread_row + PART).astype(BF)
    for s in range(STEPS):
        move_wait(s, r_sem.at[6 + s])
        attended = dot(mov_r[s, 0], place0) + dot(mov_r[s, 1], place1)
        value = res_r[:, s, :] + attended
        hid[s] = value
        squares = jnp.sum(jnp.where(lane < SLICE, value * value, 0.0), axis=1, keepdims=True)
        squares_hi = squares.astype(BF).astype(F32)
        value_hi = value.astype(BF).astype(F32)
        scaled = value * gain_ref[l]
        scaled = jnp.where(lane == SS_LANE, squares_hi, scaled)
        scaled = jnp.where(lane == SS_LANE + 1, squares - squares_hi, scaled)
        in_hi = jnp.logical_and(lane >= SHARE_HI, lane < SHARE_HI + EXPERTS)
        in_lo = jnp.logical_and(lane >= SHARE_LO, lane < SHARE_LO + EXPERTS)
        scaled = jnp.where(in_hi, value_hi, scaled)
        scaled = jnp.where(in_lo, value - value_hi, scaled)
        rows[s, e] = scaled.astype(BF)
        gather_start(rows.at[s], 8 + s, xy_sem.at[s], r_sem.at[8 + s])

    wait_bytes(w_r.at[pl.ds(0, NE - 1)], r_sem.at[3])
    pn, pm = iota((LANES, LANES), 0), iota((LANES, LANES), 1)
    pick = jnp.logical_and(pn < SLICE, pm == pn + 2 * (pn // 14)).astype(BF)
    for mat in range(3):
        natural = dot(pick, w_r[:, 16 * mat : 16 * mat + 16, :].reshape(LANES, 256)).astype(BF)
        if mat == 2:
            w_n[2] = natural
        else:
            for half in range(2):
                w_n[half, :, 128 * mat : 128 * mat + 128] = natural[:, 128 * half : 128 * half + 128]

    ones_at = iota((16, LANES), 1)
    stat_row = jnp.logical_or(ones_at == SS_LANE, ones_at == SS_LANE + 1).astype(BF)
    tail = iota((tokens, 128), 1) + 384
    mine = jnp.logical_or(tail == SHARE_HI + e // 4, tail == SHARE_LO + e // 4)
    for s in range(STEPS):
        gather_finish(rows.at[s], 8 + s, xy_sem.at[s], r_sem.at[8 + s])
        flat = rows[s].reshape(tokens, LANES)
        gate_s[s] = dot(flat, w_n[1 - c]).astype(BF)
        remote(gate_s.at[s], gate_r.at[s], s_sem.at[10 + s], r_sem.at[10 + s], sib).start()
        stat = dot_t(stat_row, flat)
        for t in range(4):
            sq_s[s, t] = stat[0:1, 128 * t : 128 * t + 128]
        remote(sq_s.at[s], sq_r.at[s], s_sem.at[12 + s], r_sem.at[12 + s], sib).start()
        gate_o[s] = dot(flat, w_n[c])
        share[s] = jnp.sum(jnp.where(mine, flat[:, 384:].astype(F32), 0.0), axis=1, keepdims=True)

    def z_peer(k):
        t = lax.rem(z + k, NZ)
        return t, {"learn": 2 * t + c}

    for s in range(STEPS):
        wait_bytes(gate_r.at[s], r_sem.at[10 + s])
        wait_bytes(sq_r.at[s], r_sem.at[12 + s])
        sum_s[s] = (gate_o[s] + gate_r[s].astype(F32)).astype(BF).reshape(NZ, 64, 256)
        sq_t[s] = sq_s[s] + sq_r[s]
        sum_r[s, z] = sum_s[s, z]
        sq_z[s, z] = sq_t[s, z // 2]

        def send_sum(k, carry):
            t, device = z_peer(k)
            remote(sq_t.at[s, t // 2], sq_z.at[s, z], s_sem.at[16 + s], r_sem.at[16 + s], device).start()
            remote(sum_s.at[s, t], sum_r.at[s, z], s_sem.at[14 + s], r_sem.at[14 + s], device).start()
            return carry

        lax.fori_loop(1, NZ, send_sum, 0)

    sq_row, sq_lane = iota((64, 128), 0), iota((64, 128), 1)
    own_lane = sq_lane == sq_row + 64 * lax.rem(z, 2)
    for s in range(STEPS):
        wait_bytes(sum_r.at[s, pl.ds(0, NZ - 1)], r_sem.at[14 + s])
        wait_bytes(sq_z.at[s, pl.ds(0, NZ - 1)], r_sem.at[16 + s])
        total = sum_r[s, 0].astype(F32)
        squares = sq_z[s, 0]
        for k in range(1, NZ):
            total = total + sum_r[s, k].astype(F32)
            squares = squares + sq_z[s, k]
        mean = jnp.sum(jnp.where(own_lane, squares, 0.0), axis=1, keepdims=True) / WIDTH
        total = total * lax.rsqrt(mean + norm_epsilon)
        gate, up = total[:, :128], total[:, 128:]
        acts[s, c, z] = (gate / (1.0 + jnp.exp(-gate)) * up).astype(BF)

        def send_act(k, carry):
            t, device = z_peer(k)
            remote(acts.at[s, c, z], acts.at[s, c, z], s_sem.at[18 + s], r_sem.at[18 + s], device).start()
            return carry

        lax.fori_loop(1, NZ, send_act, 0)

    for s in range(STEPS):
        wait_bytes(acts.at[s, c, pl.ds(0, NZ - 1)], r_sem.at[18 + s])
        remote(acts.at[s, c], acts.at[s, c], s_sem.at[20 + s], r_sem.at[20 + s], sib).start()

    for s in range(STEPS):
        wait_bytes(acts.at[s, 1 - c], r_sem.at[20 + s])
        act = jnp.concatenate(
            [acts[s, 0].reshape(tokens, 128), acts[s, 1].reshape(tokens, 128)], axis=1
        )
        down_s[s] = (dot_t(act, w_n[2]) * share[s]).astype(BF).reshape(NX, 128, LANES)
        down_r[s, x] = down_s[s, x]

        def send_down(k, carry):
            t = lax.rem(x + k, NX)
            remote(
                down_s.at[s, t], down_r.at[s, x], s_sem.at[22 + s], r_sem.at[22 + s], {"ep": t * NY + y}
            ).start()
            return carry

        lax.fori_loop(1, NX, send_down, 0)

    for s in range(STEPS):
        wait_bytes(down_r.at[s, pl.ds(0, NX - 1)], r_sem.at[22 + s])
        total = down_r[s, 0].astype(F32)
        for k in range(1, NX):
            total = total + down_r[s, k].astype(F32)
        y_s[s] = total.astype(BF).reshape(NY, 16, LANES)
        y_r[s, y] = y_s[s, y]

        def send_y(k, carry):
            t = lax.rem(y + k, NY)
            remote(
                y_s.at[s, t], y_r.at[s, y], s_sem.at[24 + s], r_sem.at[24 + s], {"ep": x * NY + t}
            ).start()
            return carry

        lax.fori_loop(1, NY, send_y, 0)

    for s in range(STEPS):
        wait_bytes(y_r.at[s, pl.ds(0, NY - 1)], r_sem.at[24 + s])
        total = hid[s]
        routed = y_r[s, 0].astype(F32)
        for k in range(1, NY):
            routed = routed + y_r[s, k].astype(F32)
        fin_s[:, s, :] = total + routed


    def send_fin(k, carry):
        t = lax.rem(l + k, NL)
        remote(fin_s.at[t], fin_r.at[l], s_sem.at[26], r_sem.at[26], {"learn": t}).start()
        return carry

    lax.fori_loop(1, NL, send_fin, 0)
    fin_r[l] = fin_s[l]
    wait_bytes(fin_r.at[pl.ds(0, NL - 1)], r_sem.at[26])
    out_ref[...] = fin_r[...]

    wait_bytes(res_r.at[pl.ds(0, NL - 1)], s_sem.at[0])
    wait_bytes(w_r.at[pl.ds(0, NE - 1)], s_sem.at[3])
    wait_bytes(fin_r.at[pl.ds(0, NL - 1)], s_sem.at[26])
    for s in range(STEPS):
        wait_bytes(heads.at[s, pl.ds(0, NE - 1)], s_sem.at[1 + s])
        wait_bytes(att_r.at[s, pl.ds(0, NL - 1)], s_sem.at[4 + s])
        move_wait(s, s_sem.at[6 + s])
        wait_bytes(rows.at[s, pl.ds(0, NE - 1)], s_sem.at[8 + s])
        wait_bytes(gate_s.at[s], s_sem.at[10 + s])
        wait_bytes(sq_s.at[s], s_sem.at[12 + s])
        wait_bytes(sum_s.at[s, pl.ds(0, NZ - 1)], s_sem.at[14 + s])
        wait_bytes(sq_z.at[s, pl.ds(0, NZ - 1)], s_sem.at[16 + s])
        wait_bytes(acts.at[s, 0, pl.ds(0, NZ - 1)], s_sem.at[18 + s])
        wait_bytes(acts.at[s, 0], s_sem.at[20 + s])
        wait_bytes(down_s.at[s, pl.ds(0, NX - 1)], s_sem.at[22 + s])
        wait_bytes(y_s.at[s, pl.ds(0, NY - 1)], s_sem.at[24 + s])


def layer(q, kk, lens, uv, ow, res, gain, ws):
    vmem = pl.BlockSpec(memory_space=pltpu.VMEM)
    scratch = [
        pltpu.VMEM((2, NE, 16, 256), BF),
        pltpu.VMEM((2, NL, 32, 256), BF),
        pltpu.VMEM((2, NL, 32, 256), BF),
        pltpu.VMEM((2, 2, 16, 256), BF),
        pltpu.VMEM((2, 2, 16, 256), BF),
        pltpu.VMEM((NL, 2, LANES), F32),
        pltpu.VMEM((2, 16, LANES), F32),
        pltpu.VMEM((2, NE, 16, LANES), BF),
        pltpu.VMEM((NE, 48, 256), BF),
        pltpu.VMEM((3, LANES, 256), BF),
        pltpu.VMEM((2, 512, 256), BF),
        pltpu.VMEM((2, 512, 256), F32),
        pltpu.VMEM((2, 512, 256), BF),
        pltpu.VMEM((2, NZ, 64, 256), BF),
        pltpu.VMEM((2, NZ, 64, 256), BF),
        pltpu.VMEM((2, 4, 1, 128), F32),
        pltpu.VMEM((2, 4, 1, 128), F32),
        pltpu.VMEM((2, 4, 1, 128), F32),
        pltpu.VMEM((2, NZ, 1, 128), F32),
        pltpu.VMEM((2, 2, NZ, 64, 128), BF),
        pltpu.VMEM((2, NX, 128, LANES), BF),
        pltpu.VMEM((2, NX, 128, LANES), BF),
        pltpu.VMEM((2, NY, 16, LANES), BF),
        pltpu.VMEM((2, NY, 16, LANES), BF),
        pltpu.VMEM((NL, 2, LANES), F32),
        pltpu.VMEM((NL, 2, LANES), F32),
        pltpu.VMEM((2, 512, 1), F32),
        pltpu.SemaphoreType.DMA((27,)),
        pltpu.SemaphoreType.DMA((27,)),
        pltpu.SemaphoreType.DMA((2, NY)),
        pltpu.SemaphoreType.DMA((2, NY)),
    ]
    return pl.pallas_call(
        layer_kernel,
        out_shape=jax.ShapeDtypeStruct((NL, 2, LANES), F32),
        in_specs=[vmem] * 8,
        out_specs=vmem,
        scratch_shapes=scratch,
        compiler_params=pltpu.CompilerParams(
            collective_id=0, has_side_effects=True, vmem_limit_bytes=48 * 2**20
        ),
        name="decode_layer",
    )(q, kk, lens, uv, ow, res, gain, ws)


def expert_shares(expert_ids, route_weight):
    route_share = route_weight / jnp.sum(route_weight, axis=-1, keepdims=True) * route_scale
    hit = (expert_ids[..., None] == jnp.arange(EXPERTS)).astype(F32)
    return jnp.sum(route_share[..., None] * hit, axis=-2)


def per_device(
    master_weight, gradient, first_moment, second_moment, block_slot, queries, kv_cache, new_latent,
    lengths, uv_weight, out_weight, residual, norm_gain, expert_ids, route_weight,
):
    ws = adam_blocks(master_weight, gradient, first_moment, second_moment, block_slot)
    q = jnp.transpose(queries, (0, 2, 1, 3)).reshape(64, 576)
    kk = jnp.concatenate([kv_cache.reshape(16 * CACHE, 576), new_latent.reshape(32, 576)], axis=0)
    lens = jnp.tile(lengths, 4).reshape(64, 1)
    ow = jnp.pad(out_weight.reshape(256, PART), ((0, 0), (0, 256 - PART)))
    shares = expert_shares(expert_ids[:, 0], route_weight[:, 0])
    gap = jnp.zeros((2, 8), F32)
    tail = jnp.concatenate([gap, shares, shares, gap, gap, gap, gap, gap], axis=1)
    res = jnp.concatenate(
        [
            jnp.transpose(residual.astype(F32).reshape(2, NL, SLICE), (1, 0, 2)),
            jnp.broadcast_to(tail[None], (NL, 2, LANES - SLICE)),
        ],
        axis=2,
    )
    gain = jnp.pad(norm_gain.reshape(NL, 1, SLICE), ((0, 0), (0, 0), (0, LANES - SLICE)))
    out = layer(q, kk, lens, uv_weight, ow, res, gain, ws)
    return jnp.transpose(out[:, :, :SLICE], (1, 0, 2)).reshape(2, 1, WIDTH).astype(BF)


def solution(mesh):
    in_specs = (
        P(("learn", "ep"), None, None, None),
        P(("learn", "ep"), None, None, None),
        P(("learn", "ep"), None, None, None),
        P(("learn", "ep"), None, None, None),
        P(),
        P(None, "ep", "learn", None),
        P("ep", None, None),
        P(None, "ep", None),
        P("ep"),
        P("learn", None, None),
        P("learn", None, "ep"),
        P(None, ("learn", "ep"), None),
        P(),
        P(None, ("learn", "ep"), None),
        P(None, ("learn", "ep"), None),
    )
    out_specs = P(None, ("learn", "ep"), None)
    return jax.shard_map(
        per_device, mesh=mesh, in_specs=in_specs, out_specs=out_specs, check_vma=False
    )
```

```python
import functools

import jax
import jax.numpy as jnp
from jax import lax
from jax.experimental import pallas as pl
from jax.experimental.pallas import tpu as pltpu
from jax.sharding import PartitionSpec as P

BF = jnp.bfloat16
F32 = jnp.float32
MESH = pl.DeviceIdType.MESH

beta_one = 0.9
beta_two = 0.95
learn_rate = 0.01
adam_step = 50
adam_epsilon = 1e-08
norm_epsilon = 1e-06
route_scale = 2.827

NX, NY, NZ, NL, NE = 4, 8, 8, 16, 32
WIDTH, SLICE, PART = 7168, 448, 224
LANES = 512
SS_LANE, SHARE_HI, SHARE_LO = 448, 456, 464
EXPERTS, STEPS, CACHE, LAT = 8, 2, 24, 512


def dot(a, b):
    return jnp.dot(a, b, preferred_element_type=F32)


def dot_t(a, b):
    return lax.dot_general(a, b, (((1,), (1,)), ((), ())), preferred_element_type=F32)


def iota(shape, dim):
    return lax.broadcasted_iota(jnp.int32, shape, dim)


def wait_bytes(ref, sem):
    pltpu.make_async_copy(ref, ref, sem).wait()


def remote(src, dst, ssem, rsem, device):
    return pltpu.make_async_remote_copy(
        src_ref=src, dst_ref=dst, send_sem=ssem, recv_sem=rsem, device_id=device, device_id_type=MESH
    )


def column(row, size):
    count = row.shape[1]
    hit = lax.rem(iota((size, count), 0), count) == iota((size, count), 1)
    return jnp.sum(jnp.where(hit, row, jnp.zeros_like(row)), axis=1, keepdims=True)


def layer_kernel(
    mw_in, gr_in, fm_in, sm_in, slot_in, q_in, kv_in, new_in, len_in, uv_in, ow_in,
    residual_in, gain_in, ids_in, route_in, out_ref,
    mw, gr, fm, sm, slot_ref, q_ref, kv_ref, new_ref, len_ref, uv_ref, ow_ref,
    residual_ref, gain_ref, ids_ref, route_ref,
    w_s, heads, att_s, att_r, mov_s, mov_r, res_s, res_r, hid, rows, w_r, w_n,
    gate_s, gate_o, gate_r, sum_s, sum_r, sq_s, sq_r, sq_t, sq_z, acts, down_s, down_r,
    y_s, y_r, fin_s, fin_r, share,
    s_sem, r_sem, hy_sem, xy_sem, down_sem, l_sem,
):
    l = lax.axis_index("learn")
    e = lax.axis_index("ep")
    x, y = e // NY, lax.rem(e, NY)
    z, c = l // 2, lax.rem(l, 2)
    sib = {"learn": l + 1 - 2 * c}

    pairs = (
        (q_in, q_ref), (kv_in, kv_ref), (new_in, new_ref), (len_in, len_ref), (uv_in, uv_ref),
        (residual_in, residual_ref), (ids_in, ids_ref), (route_in, route_ref), (ow_in, ow_ref),
        (slot_in, slot_ref), (gain_in, gain_ref), (mw_in, mw), (gr_in, gr), (fm_in, fm), (sm_in, sm),
    )
    loads = [pltpu.make_async_copy(src, dst, l_sem.at[i]) for i, (src, dst) in enumerate(pairs)]
    for load in loads[:11]:
        load.start()

    barrier = pltpu.get_barrier_semaphore()

    def greet_ep(k, carry):
        pl.semaphore_signal(barrier, inc=1, device_id={"ep": lax.rem(e + k, NE)}, device_id_type=MESH)
        return carry

    def greet_learn(k, carry):
        pl.semaphore_signal(barrier, inc=1, device_id={"learn": lax.rem(l + k, NL)}, device_id_type=MESH)
        return carry

    lax.fori_loop(1, NE, greet_ep, 0)
    lax.fori_loop(1, NL, greet_learn, 0)
    own_move = e // 2 == l
    for j in range(2):
        @pl.when(jnp.logical_not(jnp.logical_and(own_move, lax.rem(e, 2) == j)))
        def _():
            pl.semaphore_signal(
                barrier, inc=1, device_id={"learn": e // 2, "ep": 2 * l + j}, device_id_type=MESH
            )

    for load in loads[:5]:
        load.wait()
    for load in loads[11:]:
        load.start()

    cached = 16 * CACHE
    scale = 192.0 ** (-0.5)
    parts = []
    for s in range(STEPS):
        wide = q_ref[s].astype(F32)
        for h in range(2):
            parts.append(wide[:, h, :].astype(BF))
    q = jnp.concatenate(parts, axis=0)
    old, new = kv_ref[...], new_ref[...]
    old_score, new_score = dot_t(q, old) * scale, dot_t(q, new) * scale
    row, col = iota((64, cached), 0), iota((64, cached), 1)
    first = lax.rem(row, 16) * CACHE
    live = jnp.logical_and(col >= first, col < first + column(len_ref[...], 64))
    old_score = jnp.where(live, old_score, -1e30)
    row, col = iota((64, 32), 0), iota((64, 32), 1)
    live = jnp.logical_and(lax.rem(row, 16) == lax.rem(col, 16), jnp.logical_or(col < 16, row >= 32))
    new_score = jnp.where(live, new_score, -1e30)
    top = jnp.maximum(
        jnp.max(old_score, axis=1, keepdims=True), jnp.max(new_score, axis=1, keepdims=True)
    )
    old_score, new_score = jnp.exp(old_score - top), jnp.exp(new_score - top)
    norm = jnp.sum(old_score, axis=1, keepdims=True) + jnp.sum(new_score, axis=1, keepdims=True)
    latent = dot((old_score / norm).astype(BF), old[:, :LAT])
    latent = (latent + dot((new_score / norm).astype(BF), new[:, :LAT])).astype(BF)
    for s in range(STEPS):
        for h in range(2):
            start = s * 32 + h * 16
            heads[s, e, :, 128 * h : 128 * h + 128] = dot(
                latent[start : start + 16], uv_ref[h]
            ).astype(BF)

    def gather_start(buf, i, ysem, xsem):
        def send_y(k, carry):
            t = x * NY + lax.rem(y + k, NY)
            remote(buf.at[e], buf.at[e], s_sem.at[i], ysem.at[k], {"ep": t}).start()
            return carry

        def send_x(k, carry):
            t = lax.rem(x + k, NX) * NY + y
            remote(buf.at[e], buf.at[e], s_sem.at[i], xsem, {"ep": t}).start()
            return carry

        lax.fori_loop(1, NY, send_y, 0)
        lax.fori_loop(1, NX, send_x, 0)

    def gather_relay(buf, i, ysem, xsem):
        def relay(t, carry):
            half = t // 2
            k = jnp.where(lax.rem(t, 2) == 0, half + 1, NY - 1 - half)
            o = x * NY + lax.rem(y + NY - k, NY)
            wait_bytes(buf.at[o], ysem.at[k])

            def send_x(j, carry2):
                d = lax.rem(x + j, NX) * NY + y
                remote(buf.at[o], buf.at[o], s_sem.at[i], xsem, {"ep": d}).start()
                return carry2

            return lax.fori_loop(1, NX, send_x, carry)

        lax.fori_loop(0, NY - 1, relay, 0)

    def heads_start(s):
        gather_start(heads.at[s], 1 + s, hy_sem.at[s], r_sem.at[1 + s])

    pl.semaphore_wait(barrier, NE - 1 + NL - 1 + 2 - own_move.astype(jnp.int32))
    for s in range(STEPS):
        heads_start(s)

    for load in loads[5:]:
        load.wait()
    lane8 = iota((8, LANES - SLICE), 1)
    hi_expert, lo_expert = lane8 - (SHARE_HI - SLICE), lane8 - (SHARE_LO - SLICE)
    tails = []
    for s in range(STEPS):
        ids = column(ids_ref[s], 8)
        weight = route_ref[s]
        route = column(weight / jnp.sum(weight, axis=1, keepdims=True) * route_scale, 8)
        hit = jnp.logical_or(
            jnp.logical_and(ids == hi_expert, hi_expert < EXPERTS),
            jnp.logical_and(ids == lo_expert, lo_expert < EXPERTS),
        )
        tails.append(jnp.sum(jnp.where(hit, route, 0.0), axis=0, keepdims=True))
    tail = jnp.concatenate(tails, axis=0)
    lines = residual_ref[...].astype(F32)
    for k in range(NL):
        res_s[k] = jnp.concatenate([lines[:, SLICE * k : SLICE * k + SLICE], tail], axis=1)
    res_r[l] = res_s[l]

    def send_res(k, carry):
        t = lax.rem(l + k, NL)
        remote(res_s.at[t], res_r.at[l], s_sem.at[0], r_sem.at[0], {"learn": t}).start()
        return carry

    lax.fori_loop(1, NL, send_res, 0)

    depth = mw.shape[0]
    count = depth * NE
    slots = column(slot_ref[...], NE).astype(F32)
    fits = lax.rem(iota((NE, count), 1), NE) == iota((NE, count), 0)
    slot_row = jnp.sum(jnp.where(fits, slots, 0.0), axis=0, keepdims=True).astype(jnp.int32)
    out_row, in_row = iota((NE * 16, count), 0), iota((NE * 16, count), 1)
    order = jnp.logical_and(out_row // 16 == slot_row, lax.rem(out_row, 16) == in_row // NE).astype(BF)
    first_scale = learn_rate / (1.0 - beta_one**adam_step)
    second_scale = 1.0 / (1.0 - beta_two**adam_step)
    for mat in range(3):
        g = gr[:, mat].astype(F32)
        first_new = beta_one * fm[:, mat].astype(F32) + (1.0 - beta_one) * g
        second_new = beta_two * sm[:, mat].astype(F32) + (1.0 - beta_two) * g * g
        stride = first_new * first_scale / (jnp.sqrt(second_new * second_scale) + adam_epsilon)
        updated = (mw[:, mat] - stride).astype(BF).reshape(count, 256)
        w_s[:, 16 * mat : 16 * mat + 16, :] = dot(order, updated).reshape(NE, 16, 256).astype(BF)

    w_r[e] = w_s[e]

    def send_w(k, carry):
        t = lax.rem(e + k, NE)
        remote(w_s.at[t], w_r.at[e], s_sem.at[3], r_sem.at[3], {"ep": t}).start()
        return carry

    tokens = 512
    n, m = iota((tokens, tokens), 0), iota((tokens, tokens), 1)
    reorder = (m == 32 * lax.rem(n, 16) + n // 16).astype(BF)

    def heads_relay(s):
        gather_relay(heads.at[s], 1 + s, hy_sem.at[s], r_sem.at[1 + s])

    def project(s):
        wait_bytes(heads.at[s, pl.ds(0, NE - NY)], r_sem.at[1 + s])
        ordered = dot(reorder, heads[s].reshape(tokens, 256)).astype(BF)
        projected = dot_t(ordered[:, :128], ow_ref[0]) + dot_t(ordered[:, 128:], ow_ref[1])
        att_s[s] = projected.astype(BF).reshape(NL, 32, PART)
        att_r[s, l] = att_s[s, l]

        def send_att(k, carry):
            t = lax.rem(l + k, NL)
            remote(att_s.at[s, t], att_r.at[s, l], s_sem.at[4 + s], r_sem.at[4 + s], {"learn": t}).start()
            return carry

        lax.fori_loop(1, NL, send_att, 0)

    def move(s):
        wait_bytes(att_r.at[s, pl.ds(0, NL - 1)], r_sem.at[4 + s])
        total = att_r[s, 0].astype(F32)
        for k in range(1, NL):
            total = total + att_r[s, k].astype(F32)
        mov_s[s] = total.astype(BF).reshape(2, 16, PART)
        for j in range(2):
            here = jnp.logical_and(own_move, lax.rem(e, 2) == j)

            @pl.when(here)
            def _():
                mov_r[s, lax.rem(e, 2)] = mov_s[s, j]

            @pl.when(jnp.logical_not(here))
            def _():
                remote(
                    mov_s.at[s, j], mov_r.at[s, lax.rem(e, 2)], s_sem.at[6 + s], r_sem.at[6 + s],
                    {"learn": e // 2, "ep": 2 * l + j},
                ).start()

    def move_wait(s, sem):
        @pl.when(own_move)
        def _():
            wait_bytes(mov_r.at[s, 0], sem)

        @pl.when(jnp.logical_not(own_move))
        def _():
            wait_bytes(mov_r.at[s], sem)

    gains = gain_ref[pl.ds(7 * z, 7), :]
    even = jnp.concatenate([gains[k : k + 1] for k in range(4)], axis=1)
    odd = jnp.concatenate([gains[k : k + 1] for k in range(3, 7)], axis=1)
    odd = jnp.concatenate([odd[:, 64:], odd[:, :64]], axis=1)
    gain = jnp.where(c == 0, even, odd)
    lane = iota((16, LANES), 1)
    spread_row, spread_col = iota((PART, LANES), 0), iota((PART, LANES), 1)
    place0 = (spread_col == spread_row).astype(BF)
    place1 = (spread_col == spread_row + PART).astype(BF)

    def rows_start(s):
        move_wait(s, r_sem.at[6 + s])
        attended = dot(mov_r[s, 0], place0) + dot(mov_r[s, 1], place1)
        value = res_r[:, s, :] + attended
        hid[s] = value
        squares = jnp.sum(jnp.where(lane < SLICE, value * value, 0.0), axis=1, keepdims=True)
        squares_hi = squares.astype(BF).astype(F32)
        value_hi = value.astype(BF).astype(F32)
        scaled = value * gain
        scaled = jnp.where(lane == SS_LANE, squares_hi, scaled)
        scaled = jnp.where(lane == SS_LANE + 1, squares - squares_hi, scaled)
        in_hi = jnp.logical_and(lane >= SHARE_HI, lane < SHARE_HI + EXPERTS)
        in_lo = jnp.logical_and(lane >= SHARE_LO, lane < SHARE_LO + EXPERTS)
        scaled = jnp.where(in_hi, value_hi, scaled)
        scaled = jnp.where(in_lo, value - value_hi, scaled)
        rows[s, e] = scaled.astype(BF)
        gather_start(rows.at[s], 8 + s, xy_sem.at[s], r_sem.at[8 + s])

    def arrange():
        wait_bytes(w_r.at[pl.ds(0, NE - 1)], r_sem.at[3])
        pn, pm = iota((LANES, LANES), 0), iota((LANES, LANES), 1)
        pick = jnp.logical_and(pn < SLICE, pm == pn + 2 * (pn // 14)).astype(BF)
        for mat in range(3):
            natural = dot(pick, w_r[:, 16 * mat : 16 * mat + 16, :].reshape(LANES, 256)).astype(BF)
            if mat == 2:
                w_n[2] = natural
            else:
                for half in range(2):
                    w_n[half, :, 128 * mat : 128 * mat + 128] = natural[:, 128 * half : 128 * half + 128]

    ones_at = iota((16, LANES), 1)
    stat_row = jnp.logical_or(ones_at == SS_LANE, ones_at == SS_LANE + 1).astype(BF)
    tail_lane = iota((tokens, 128), 1) + 384
    mine = jnp.logical_or(tail_lane == SHARE_HI + e // 4, tail_lane == SHARE_LO + e // 4)

    def rows_relay(s):
        gather_relay(rows.at[s], 8 + s, xy_sem.at[s], r_sem.at[8 + s])

    def gate(s):
        wait_bytes(rows.at[s, pl.ds(0, NE - NY)], r_sem.at[8 + s])
        flat = rows[s].reshape(tokens, LANES)
        gate_s[s] = dot(flat, w_n[1 - c]).astype(BF)
        remote(gate_s.at[s], gate_r.at[s], s_sem.at[10 + s], r_sem.at[10 + s], sib).start()
        stat = dot_t(stat_row, flat)
        for t in range(4):
            sq_s[s, t] = stat[0:1, 128 * t : 128 * t + 128]
        remote(sq_s.at[s], sq_r.at[s], s_sem.at[12 + s], r_sem.at[12 + s], sib).start()
        gate_o[s] = dot(flat, w_n[c])
        share[s] = jnp.sum(jnp.where(mine, flat[:, 384:].astype(F32), 0.0), axis=1, keepdims=True)

    def z_peer(k):
        t = lax.rem(z + k, NZ)
        return t, {"learn": 2 * t + c}

    def pair_sum(s):
        wait_bytes(gate_r.at[s], r_sem.at[10 + s])
        wait_bytes(sq_r.at[s], r_sem.at[12 + s])
        sum_s[s] = (gate_o[s] + gate_r[s].astype(F32)).astype(BF).reshape(NZ, 64, 256)
        sq_t[s] = sq_s[s] + sq_r[s]
        sum_r[s, z] = sum_s[s, z]
        sq_z[s, z] = sq_t[s, z // 2]

        def send_sum(k, carry):
            t, device = z_peer(k)
            remote(sq_t.at[s, t // 2], sq_z.at[s, z], s_sem.at[16 + s], r_sem.at[16 + s], device).start()
            remote(sum_s.at[s, t], sum_r.at[s, z], s_sem.at[14 + s], r_sem.at[14 + s], device).start()
            return carry

        lax.fori_loop(1, NZ, send_sum, 0)

    sq_row, sq_lane = iota((64, 128), 0), iota((64, 128), 1)
    own_lane = sq_lane == sq_row + 64 * lax.rem(z, 2)

    def activate(s):
        wait_bytes(sum_r.at[s, pl.ds(0, NZ - 1)], r_sem.at[14 + s])
        wait_bytes(sq_z.at[s, pl.ds(0, NZ - 1)], r_sem.at[16 + s])
        total = sum_r[s, 0].astype(F32)
        squares = sq_z[s, 0]
        for k in range(1, NZ):
            total = total + sum_r[s, k].astype(F32)
            squares = squares + sq_z[s, k]
        mean = jnp.sum(jnp.where(own_lane, squares, 0.0), axis=1, keepdims=True) / WIDTH
        total = total * lax.rsqrt(mean + norm_epsilon)
        gated, up = total[:, :128], total[:, 128:]
        acts[s, c, z] = (gated / (1.0 + jnp.exp(-gated)) * up).astype(BF)

        def send_act(k, carry):
            t, device = z_peer(k)
            remote(acts.at[s, c, z], acts.at[s, c, z], s_sem.at[18 + s], r_sem.at[18 + s], device).start()
            return carry

        lax.fori_loop(1, NZ, send_act, 0)

    def pair_acts(s):
        wait_bytes(acts.at[s, c, pl.ds(0, NZ - 1)], r_sem.at[18 + s])
        remote(acts.at[s, c], acts.at[s, c], s_sem.at[20 + s], r_sem.at[20 + s], sib).start()

    def down(s):
        wait_bytes(acts.at[s, 1 - c], r_sem.at[20 + s])
        act = jnp.concatenate(
            [acts[s, 0].reshape(tokens, 128), acts[s, 1].reshape(tokens, 128)], axis=1
        )
        down_s[s] = (dot_t(act, w_n[2]) * share[s]).astype(BF).reshape(NX, 128, LANES)
        down_r[s, x] = down_s[s, x]

        def send_down(k, carry):
            t = lax.rem(x + lax.rem(k, NX - 1) + 1, NX)
            part = pl.ds(pl.multiple_of(k // (NX - 1) * 64, 64), 64)
            remote(
                down_s.at[s, t, part], down_r.at[s, x, part], s_sem.at[22 + s],
                down_sem.at[s, k // (NX - 1)], {"ep": t * NY + y},
            ).start()
            return carry

        lax.fori_loop(0, 2 * (NX - 1), send_down, 0)

    def sum_x(s, half):
        part = pl.ds(64 * half, 64)
        wait_bytes(down_r.at[s, pl.ds(0, NX - 1), part], down_sem.at[s, half])
        total = down_r[s, 0, part].astype(F32)
        for k in range(1, NX):
            total = total + down_r[s, k, part].astype(F32)
        y_s[s, pl.ds(4 * half, 4)] = total.astype(BF).reshape(4, 16, LANES)
        for t in range(4 * half, 4 * half + 4):
            @pl.when(y == t)
            def _():
                y_r[s, t] = y_s[s, t]

            @pl.when(y != t)
            def _():
                remote(
                    y_s.at[s, t], y_r.at[s, y], s_sem.at[24 + s], r_sem.at[24 + s], {"ep": x * NY + t}
                ).start()

    def sum_y(s):
        wait_bytes(y_r.at[s, pl.ds(0, NY - 1)], r_sem.at[24 + s])
        routed = y_r[s, 0].astype(F32)
        for k in range(1, NY):
            routed = routed + y_r[s, k].astype(F32)
        fin_s[:, s, :] = hid[s] + routed

    heads_relay(0)
    heads_relay(1)
    lax.fori_loop(1, NE, send_w, 0)
    project(0)
    project(1)
    move(0)
    wait_bytes(res_r.at[pl.ds(0, NL - 1)], r_sem.at[0])
    rows_start(0)
    move(1)
    rows_relay(0)
    rows_start(1)
    arrange()
    gate(0)
    rows_relay(1)
    pair_sum(0)
    gate(1)
    activate(0)
    pair_sum(1)
    pair_acts(0)
    down(0)
    activate(1)
    sum_x(0, 0)
    sum_x(0, 1)
    pair_acts(1)
    down(1)
    sum_y(0)
    sum_x(1, 0)
    sum_x(1, 1)
    sum_y(1)

    def send_fin(k, carry):
        t = lax.rem(l + k, NL)
        remote(fin_s.at[t], fin_r.at[l], s_sem.at[26], r_sem.at[26], {"learn": t}).start()
        return carry

    lax.fori_loop(1, NL, send_fin, 0)
    fin_r[l] = fin_s[l]
    wait_bytes(fin_r.at[pl.ds(0, NL - 1)], r_sem.at[26])
    for k in range(NL):
        out_ref[:, SLICE * k : SLICE * k + SLICE] = fin_r[k][:, :SLICE]

    wait_bytes(res_r.at[pl.ds(0, NL - 1)], s_sem.at[0])
    wait_bytes(w_r.at[pl.ds(0, NE - 1)], s_sem.at[3])
    wait_bytes(fin_r.at[pl.ds(0, NL - 1)], s_sem.at[26])
    for s in range(STEPS):
        wait_bytes(heads.at[s, pl.ds(0, NE - 1)], s_sem.at[1 + s])
        wait_bytes(att_r.at[s, pl.ds(0, NL - 1)], s_sem.at[4 + s])
        move_wait(s, s_sem.at[6 + s])
        wait_bytes(rows.at[s, pl.ds(0, NE - 1)], s_sem.at[8 + s])
        wait_bytes(gate_s.at[s], s_sem.at[10 + s])
        wait_bytes(sq_s.at[s], s_sem.at[12 + s])
        wait_bytes(sum_s.at[s, pl.ds(0, NZ - 1)], s_sem.at[14 + s])
        wait_bytes(sq_z.at[s, pl.ds(0, NZ - 1)], s_sem.at[16 + s])
        wait_bytes(acts.at[s, 0, pl.ds(0, NZ - 1)], s_sem.at[18 + s])
        wait_bytes(acts.at[s, 0], s_sem.at[20 + s])
        wait_bytes(down_s.at[s, pl.ds(0, NX - 1)], s_sem.at[22 + s])
        wait_bytes(y_s.at[s, pl.ds(0, NY - 1)], s_sem.at[24 + s])


def layer(*operands):
    anywhere = pl.BlockSpec(memory_space=pl.ANY)
    vmem = pl.BlockSpec(memory_space=pltpu.VMEM)
    scratch = [pltpu.VMEM(a.shape, a.dtype) for a in operands] + [
        pltpu.VMEM((NE, 48, 256), BF),
        pltpu.VMEM((2, NE, 16, 256), BF),
        pltpu.VMEM((2, NL, 32, PART), BF),
        pltpu.VMEM((2, NL, 32, PART), BF),
        pltpu.VMEM((2, 2, 16, PART), BF),
        pltpu.VMEM((2, 2, 16, PART), BF),
        pltpu.VMEM((NL, 2, LANES), F32),
        pltpu.VMEM((NL, 2, LANES), F32),
        pltpu.VMEM((2, 16, LANES), F32),
        pltpu.VMEM((2, NE, 16, LANES), BF),
        pltpu.VMEM((NE, 48, 256), BF),
        pltpu.VMEM((3, LANES, 256), BF),
        pltpu.VMEM((2, 512, 256), BF),
        pltpu.VMEM((2, 512, 256), F32),
        pltpu.VMEM((2, 512, 256), BF),
        pltpu.VMEM((2, NZ, 64, 256), BF),
        pltpu.VMEM((2, NZ, 64, 256), BF),
        pltpu.VMEM((2, 4, 1, 128), F32),
        pltpu.VMEM((2, 4, 1, 128), F32),
        pltpu.VMEM((2, 4, 1, 128), F32),
        pltpu.VMEM((2, NZ, 1, 128), F32),
        pltpu.VMEM((2, 2, NZ, 64, 128), BF),
        pltpu.VMEM((2, NX, 128, LANES), BF),
        pltpu.VMEM((2, NX, 128, LANES), BF),
        pltpu.VMEM((2, NY, 16, LANES), BF),
        pltpu.VMEM((2, NY, 16, LANES), BF),
        pltpu.VMEM((NL, 2, LANES), F32),
        pltpu.VMEM((NL, 2, LANES), F32),
        pltpu.VMEM((2, 512, 1), F32),
        pltpu.SemaphoreType.DMA((27,)),
        pltpu.SemaphoreType.DMA((27,)),
        pltpu.SemaphoreType.DMA((2, NY)),
        pltpu.SemaphoreType.DMA((2, NY)),
        pltpu.SemaphoreType.DMA((2, 2)),
        pltpu.SemaphoreType.DMA((15,)),
    ]
    return pl.pallas_call(
        layer_kernel,
        out_shape=jax.ShapeDtypeStruct((2, WIDTH), F32),
        in_specs=[anywhere] * len(operands),
        out_specs=vmem,
        scratch_shapes=scratch,
        compiler_params=pltpu.CompilerParams(
            collective_id=0, has_side_effects=True, vmem_limit_bytes=62 * 2**20
        ),
        name="decode_layer",
    )(*operands)


def per_device(
    master_weight, gradient, first_moment, second_moment, block_slot, queries, kv_cache, new_latent,
    lengths, uv_weight, out_weight, residual, norm_gain, expert_ids, route_weight,
):
    return layer(
        master_weight,
        gradient,
        first_moment,
        second_moment,
        block_slot.reshape(1, NE),
        queries,
        kv_cache.reshape(16 * CACHE, 576),
        new_latent.reshape(32, 576),
        lengths.reshape(1, 16),
        uv_weight,
        jnp.swapaxes(out_weight, 1, 2),
        residual.reshape(2, WIDTH),
        norm_gain.reshape(WIDTH // 128, 128),
        expert_ids,
        route_weight,
    ).reshape(2, 1, WIDTH).astype(BF)


def solution(mesh):
    in_specs = (
        P(("learn", "ep"), None, None, None),
        P(("learn", "ep"), None, None, None),
        P(("learn", "ep"), None, None, None),
        P(("learn", "ep"), None, None, None),
        P(),
        P(None, "ep", "learn", None),
        P("ep", None, None),
        P(None, "ep", None),
        P("ep"),
        P("learn", None, None),
        P("learn", None, "ep"),
        P(None, ("learn", "ep"), None),
        P(),
        P(None, ("learn", "ep"), None),
        P(None, ("learn", "ep"), None),
    )
    out_specs = P(None, ("learn", "ep"), None)
    return jax.shard_map(
        per_device, mesh=mesh, in_specs=in_specs, out_specs=out_specs, check_vma=False
    )
```

```python
import functools

import jax
import jax.numpy as jnp
from jax import lax
from jax.experimental import pallas as pl
from jax.experimental.pallas import tpu as pltpu
from jax.sharding import PartitionSpec as P

BF = jnp.bfloat16
F32 = jnp.float32
MESH = pl.DeviceIdType.MESH

beta_one = 0.9
beta_two = 0.95
learn_rate = 0.01
adam_step = 50
adam_epsilon = 1e-08
norm_epsilon = 1e-06
route_scale = 2.827

NX, NY, NZ, NL, NE = 4, 8, 8, 16, 32
WIDTH, SLICE, PART = 7168, 448, 224
LANES = 512
SS_LANE, SHARE_HI, SHARE_LO = 448, 456, 464
EXPERTS, STEPS, CACHE, LAT = 8, 2, 24, 512


def dot(a, b):
    return jnp.dot(a, b, preferred_element_type=F32)


def dot_t(a, b):
    return lax.dot_general(a, b, (((1,), (1,)), ((), ())), preferred_element_type=F32)


def iota(shape, dim):
    return lax.broadcasted_iota(jnp.int32, shape, dim)


def wait_bytes(ref, sem):
    pltpu.make_async_copy(ref, ref, sem).wait()


def remote(src, dst, ssem, rsem, device):
    return pltpu.make_async_remote_copy(
        src_ref=src, dst_ref=dst, send_sem=ssem, recv_sem=rsem, device_id=device, device_id_type=MESH
    )


def column(row, size):
    count = row.shape[1]
    hit = lax.rem(iota((size, count), 0), count) == iota((size, count), 1)
    return jnp.sum(jnp.where(hit, row, jnp.zeros_like(row)), axis=1, keepdims=True)


def layer_kernel(
    mw_in, gr_in, fm_in, sm_in, slot_in, q_in, kv_in, new_in, len_in, uv_in, ow_in,
    residual_in, gain_in, ids_in, route_in, out_ref,
    mw, gr, fm, sm, slot_ref, q_ref, kv_ref, new_ref, len_ref, uv_ref, ow_ref,
    residual_ref, gain_ref, ids_ref, route_ref,
    w_s, heads, pair_s, pair_r, att_o, att_s, att_r, mov_s, mov_r, res_s, res_r, hid, rows, w_r, w_n,
    gate_s, gate_o, gate_r, sum_s, sum_r, sq_s, sq_r, sq_t, sq_z, acts, down_s, down_r,
    y_s, y_r, fin_s, fin_r, share,
    s_sem, r_sem, hy_sem, xy_sem, down_sem, l_sem,
):
    l = lax.axis_index("learn")
    e = lax.axis_index("ep")
    x, y = e // NY, lax.rem(e, NY)
    z, c = l // 2, lax.rem(l, 2)
    sib = {"learn": l + 1 - 2 * c}

    pairs = (
        (q_in, q_ref), (kv_in, kv_ref), (new_in, new_ref), (len_in, len_ref), (uv_in, uv_ref),
        (residual_in, residual_ref), (ids_in, ids_ref), (route_in, route_ref), (ow_in, ow_ref),
        (slot_in, slot_ref), (gain_in, gain_ref), (mw_in, mw), (gr_in, gr), (fm_in, fm), (sm_in, sm),
    )
    loads = [pltpu.make_async_copy(src, dst, l_sem.at[i]) for i, (src, dst) in enumerate(pairs)]
    for load in loads[:11]:
        load.start()

    barrier = pltpu.get_barrier_semaphore()

    def greet_ep(k, carry):
        pl.semaphore_signal(barrier, inc=1, device_id={"ep": lax.rem(e + k, NE)}, device_id_type=MESH)
        return carry

    def greet_learn(k, carry):
        pl.semaphore_signal(barrier, inc=1, device_id={"learn": lax.rem(l + k, NL)}, device_id_type=MESH)
        return carry

    lax.fori_loop(1, NE, greet_ep, 0)
    lax.fori_loop(1, NL, greet_learn, 0)
    own_move = e // 2 == l
    for j in range(2):
        @pl.when(jnp.logical_not(jnp.logical_and(own_move, lax.rem(e, 2) == j)))
        def _():
            pl.semaphore_signal(
                barrier, inc=1, device_id={"learn": e // 2, "ep": 2 * l + j}, device_id_type=MESH
            )

    for load in loads[:5]:
        load.wait()
    for load in loads[11:]:
        load.start()

    cached = 16 * CACHE
    scale = 192.0 ** (-0.5)
    parts = []
    for s in range(STEPS):
        wide = q_ref[s].astype(F32)
        for h in range(2):
            parts.append(wide[:, h, :].astype(BF))
    q = jnp.concatenate(parts, axis=0)
    old, new = kv_ref[...], new_ref[...]
    old_score, new_score = dot_t(q, old) * scale, dot_t(q, new) * scale
    row, col = iota((64, cached), 0), iota((64, cached), 1)
    first = lax.rem(row, 16) * CACHE
    live = jnp.logical_and(col >= first, col < first + column(len_ref[...], 64))
    old_score = jnp.where(live, old_score, -1e30)
    row, col = iota((64, 32), 0), iota((64, 32), 1)
    live = jnp.logical_and(lax.rem(row, 16) == lax.rem(col, 16), jnp.logical_or(col < 16, row >= 32))
    new_score = jnp.where(live, new_score, -1e30)
    top = jnp.maximum(
        jnp.max(old_score, axis=1, keepdims=True), jnp.max(new_score, axis=1, keepdims=True)
    )
    old_score, new_score = jnp.exp(old_score - top), jnp.exp(new_score - top)
    norm = jnp.sum(old_score, axis=1, keepdims=True) + jnp.sum(new_score, axis=1, keepdims=True)
    latent = dot((old_score / norm).astype(BF), old[:, :LAT])
    latent = (latent + dot((new_score / norm).astype(BF), new[:, :LAT])).astype(BF)
    for s in range(STEPS):
        for h in range(2):
            start = s * 32 + h * 16
            heads[s, e, :, 128 * h : 128 * h + 128] = dot(
                latent[start : start + 16], uv_ref[h]
            ).astype(BF)

    def gather_start(buf, i, ysem, xsem):
        def send_y(k, carry):
            t = x * NY + lax.rem(y + k, NY)
            remote(buf.at[e], buf.at[e], s_sem.at[i], ysem.at[k], {"ep": t}).start()
            return carry

        def send_x(k, carry):
            t = lax.rem(x + k, NX) * NY + y
            remote(buf.at[e], buf.at[e], s_sem.at[i], xsem, {"ep": t}).start()
            return carry

        lax.fori_loop(1, NY, send_y, 0)
        lax.fori_loop(1, NX, send_x, 0)

    def gather_relay(buf, i, ysem, xsem):
        def relay(t, carry):
            half = t // 2
            k = jnp.where(lax.rem(t, 2) == 0, half + 1, NY - 1 - half)
            o = x * NY + lax.rem(y + NY - k, NY)
            wait_bytes(buf.at[o], ysem.at[k])

            def send_x(j, carry2):
                d = lax.rem(x + j, NX) * NY + y
                remote(buf.at[o], buf.at[o], s_sem.at[i], xsem, {"ep": d}).start()
                return carry2

            return lax.fori_loop(1, NX, send_x, carry)

        lax.fori_loop(0, NY - 1, relay, 0)

    def heads_start(s):
        gather_start(heads.at[s], 1 + s, hy_sem.at[s], r_sem.at[1 + s])

    pl.semaphore_wait(barrier, NE - 1 + NL - 1 + 2 - own_move.astype(jnp.int32))
    heads_start(0)

    for load in loads[5:]:
        load.wait()
    lane8 = iota((8, LANES - SLICE), 1)
    hi_expert, lo_expert = lane8 - (SHARE_HI - SLICE), lane8 - (SHARE_LO - SLICE)
    tails = []
    for s in range(STEPS):
        ids = column(ids_ref[s], 8)
        weight = route_ref[s]
        route = column(weight / jnp.sum(weight, axis=1, keepdims=True) * route_scale, 8)
        hit = jnp.logical_or(
            jnp.logical_and(ids == hi_expert, hi_expert < EXPERTS),
            jnp.logical_and(ids == lo_expert, lo_expert < EXPERTS),
        )
        tails.append(jnp.sum(jnp.where(hit, route, 0.0), axis=0, keepdims=True))
    tail = jnp.concatenate(tails, axis=0)
    lines = residual_ref[...].astype(F32)
    for k in range(NL):
        res_s[k] = jnp.concatenate([lines[:, SLICE * k : SLICE * k + SLICE], tail], axis=1)
    res_r[l] = res_s[l]

    def send_res(k, carry):
        t = lax.rem(l + k, NL)
        remote(res_s.at[t], res_r.at[l], s_sem.at[0], r_sem.at[0], {"learn": t}).start()
        return carry

    lax.fori_loop(1, NL, send_res, 0)

    depth = mw.shape[0]
    count = depth * NE
    slots = column(slot_ref[...], NE).astype(F32)
    fits = lax.rem(iota((NE, count), 1), NE) == iota((NE, count), 0)
    slot_row = jnp.sum(jnp.where(fits, slots, 0.0), axis=0, keepdims=True).astype(jnp.int32)
    out_row, in_row = iota((NE * 16, count), 0), iota((NE * 16, count), 1)
    order = jnp.logical_and(out_row // 16 == slot_row, lax.rem(out_row, 16) == in_row // NE).astype(BF)
    first_scale = learn_rate / (1.0 - beta_one**adam_step)
    second_scale = 1.0 / (1.0 - beta_two**adam_step)
    for mat in range(3):
        g = gr[:, mat].astype(F32)
        first_new = beta_one * fm[:, mat].astype(F32) + (1.0 - beta_one) * g
        second_new = beta_two * sm[:, mat].astype(F32) + (1.0 - beta_two) * g * g
        stride = first_new * first_scale / (jnp.sqrt(second_new * second_scale) + adam_epsilon)
        updated = (mw[:, mat] - stride).astype(BF).reshape(count, 256)
        w_s[:, 16 * mat : 16 * mat + 16, :] = dot(order, updated).reshape(NE, 16, 256).astype(BF)

    w_r[e] = w_s[e]

    def send_gates(k, carry):
        t = lax.rem(e + k, NE)
        remote(
            w_s.at[t, pl.ds(0, 32)], w_r.at[e, pl.ds(0, 32)], s_sem.at[3], r_sem.at[3], {"ep": t}
        ).start()
        return carry

    def send_downs(k, carry):
        t = lax.rem(e + k, NE)
        remote(
            w_s.at[t, pl.ds(32, 16)], w_r.at[e, pl.ds(32, 16)], s_sem.at[29], r_sem.at[29], {"ep": t}
        ).start()
        return carry

    tokens = 512
    n, m = iota((tokens // 2, tokens), 0), iota((tokens // 2, tokens), 1)
    group = 4 * (n // 32) + lax.rem(n // 16, 2)
    picked = m - 32 * lax.rem(n, 16) - group
    reorder_own = (picked == 2 * c).astype(BF)
    reorder_sib = (picked == 2 - 2 * c).astype(BF)

    def z_peer(k):
        t = lax.rem(z + k, NZ)
        return t, {"learn": 2 * t + c}

    def heads_relay(s):
        gather_relay(heads.at[s], 1 + s, hy_sem.at[s], r_sem.at[1 + s])

    def project(s):
        wait_bytes(heads.at[s, pl.ds(0, NE - NY)], r_sem.at[1 + s])
        flat = heads[s].reshape(tokens, 256)

        def half(order):
            ordered = dot(order, flat).astype(BF)
            return dot_t(ordered[:, :128], ow_ref[0]) + dot_t(ordered[:, 128:], ow_ref[1])

        pair_s[s] = half(reorder_sib).astype(BF)
        remote(pair_s.at[s], pair_r.at[s], s_sem.at[27 + s], r_sem.at[27 + s], sib).start()
        att_o[s] = half(reorder_own)

    def project_sum(s):
        wait_bytes(pair_r.at[s], r_sem.at[27 + s])
        att_s[s] = (att_o[s] + pair_r[s].astype(F32)).astype(BF).reshape(NZ, 32, PART)
        att_r[s, z] = att_s[s, z]

        def send_att(k, carry):
            t, device = z_peer(k)
            remote(att_s.at[s, t], att_r.at[s, z], s_sem.at[4 + s], r_sem.at[4 + s], device).start()
            return carry

        lax.fori_loop(1, NZ, send_att, 0)

    def move(s):
        wait_bytes(att_r.at[s, pl.ds(0, NZ - 1)], r_sem.at[4 + s])
        total = att_r[s, 0].astype(F32)
        for k in range(1, NZ):
            total = total + att_r[s, k].astype(F32)
        mov_s[s] = total.astype(BF).reshape(2, 16, PART)
        for j in range(2):
            here = jnp.logical_and(own_move, lax.rem(e, 2) == j)

            @pl.when(here)
            def _():
                mov_r[s, lax.rem(e, 2)] = mov_s[s, j]

            @pl.when(jnp.logical_not(here))
            def _():
                remote(
                    mov_s.at[s, j], mov_r.at[s, lax.rem(e, 2)], s_sem.at[6 + s], r_sem.at[6 + s],
                    {"learn": e // 2, "ep": 2 * l + j},
                ).start()

    def move_wait(s, sem):
        @pl.when(own_move)
        def _():
            wait_bytes(mov_r.at[s, 0], sem)

        @pl.when(jnp.logical_not(own_move))
        def _():
            wait_bytes(mov_r.at[s], sem)

    gains = gain_ref[pl.ds(7 * z, 7), :]
    even = jnp.concatenate([gains[k : k + 1] for k in range(4)], axis=1)
    odd = jnp.concatenate([gains[k : k + 1] for k in range(3, 7)], axis=1)
    odd = jnp.concatenate([odd[:, 64:], odd[:, :64]], axis=1)
    gain = jnp.where(c == 0, even, odd)
    lane = iota((16, LANES), 1)
    spread_row, spread_col = iota((PART, LANES), 0), iota((PART, LANES), 1)
    place0 = (spread_col == spread_row).astype(BF)
    place1 = (spread_col == spread_row + PART).astype(BF)

    def rows_start(s):
        move_wait(s, r_sem.at[6 + s])
        attended = dot(mov_r[s, 0], place0) + dot(mov_r[s, 1], place1)
        value = res_r[:, s, :] + attended
        hid[s] = value
        squares = jnp.sum(jnp.where(lane < SLICE, value * value, 0.0), axis=1, keepdims=True)
        squares_hi = squares.astype(BF).astype(F32)
        value_hi = value.astype(BF).astype(F32)
        scaled = value * gain
        scaled = jnp.where(lane == SS_LANE, squares_hi, scaled)
        scaled = jnp.where(lane == SS_LANE + 1, squares - squares_hi, scaled)
        in_hi = jnp.logical_and(lane >= SHARE_HI, lane < SHARE_HI + EXPERTS)
        in_lo = jnp.logical_and(lane >= SHARE_LO, lane < SHARE_LO + EXPERTS)
        scaled = jnp.where(in_hi, value_hi, scaled)
        scaled = jnp.where(in_lo, value - value_hi, scaled)
        rows[s, e] = scaled.astype(BF)
        gather_start(rows.at[s], 8 + s, xy_sem.at[s], r_sem.at[8 + s])

    pn, pm = iota((LANES, LANES), 0), iota((LANES, LANES), 1)
    pick = jnp.logical_and(pn < SLICE, pm == pn + 2 * (pn // 14)).astype(BF)

    def natural(mat):
        return dot(pick, w_r[:, 16 * mat : 16 * mat + 16, :].reshape(LANES, 256)).astype(BF)

    def arrange_gates():
        wait_bytes(w_r.at[pl.ds(0, NE - 1), pl.ds(0, 32)], r_sem.at[3])
        for mat in range(2):
            block = natural(mat)
            for half in range(2):
                w_n[half, :, 128 * mat : 128 * mat + 128] = block[:, 128 * half : 128 * half + 128]

    def arrange_downs():
        wait_bytes(w_r.at[pl.ds(0, NE - 1), pl.ds(32, 16)], r_sem.at[29])
        w_n[2] = natural(2)

    ones_at = iota((16, LANES), 1)
    stat_row = jnp.logical_or(ones_at == SS_LANE, ones_at == SS_LANE + 1).astype(BF)
    tail_lane = iota((tokens, 128), 1) + 384
    mine = jnp.logical_or(tail_lane == SHARE_HI + e // 4, tail_lane == SHARE_LO + e // 4)

    def rows_relay(s):
        gather_relay(rows.at[s], 8 + s, xy_sem.at[s], r_sem.at[8 + s])

    def gate(s):
        wait_bytes(rows.at[s, pl.ds(0, NE - NY)], r_sem.at[8 + s])
        flat = rows[s].reshape(tokens, LANES)
        gate_s[s] = dot(flat, w_n[1 - c]).astype(BF)
        remote(gate_s.at[s], gate_r.at[s], s_sem.at[10 + s], r_sem.at[10 + s], sib).start()
        stat = dot_t(stat_row, flat)
        for t in range(4):
            sq_s[s, t] = stat[0:1, 128 * t : 128 * t + 128]
        remote(sq_s.at[s], sq_r.at[s], s_sem.at[12 + s], r_sem.at[12 + s], sib).start()
        gate_o[s] = dot(flat, w_n[c])
        share[s] = jnp.sum(jnp.where(mine, flat[:, 384:].astype(F32), 0.0), axis=1, keepdims=True)

    def pair_sum(s):
        wait_bytes(gate_r.at[s], r_sem.at[10 + s])
        wait_bytes(sq_r.at[s], r_sem.at[12 + s])
        sum_s[s] = (gate_o[s] + gate_r[s].astype(F32)).astype(BF).reshape(NZ, 64, 256)
        sq_t[s] = sq_s[s] + sq_r[s]
        sum_r[s, z] = sum_s[s, z]
        sq_z[s, z] = sq_t[s, z // 2]

        def send_sum(k, carry):
            t, device = z_peer(k)
            remote(sq_t.at[s, t // 2], sq_z.at[s, z], s_sem.at[16 + s], r_sem.at[16 + s], device).start()
            remote(sum_s.at[s, t], sum_r.at[s, z], s_sem.at[14 + s], r_sem.at[14 + s], device).start()
            return carry

        lax.fori_loop(1, NZ, send_sum, 0)

    sq_row, sq_lane = iota((64, 128), 0), iota((64, 128), 1)
    own_lane = sq_lane == sq_row + 64 * lax.rem(z, 2)

    def activate(s):
        wait_bytes(sum_r.at[s, pl.ds(0, NZ - 1)], r_sem.at[14 + s])
        wait_bytes(sq_z.at[s, pl.ds(0, NZ - 1)], r_sem.at[16 + s])
        total = sum_r[s, 0].astype(F32)
        squares = sq_z[s, 0]
        for k in range(1, NZ):
            total = total + sum_r[s, k].astype(F32)
            squares = squares + sq_z[s, k]
        mean = jnp.sum(jnp.where(own_lane, squares, 0.0), axis=1, keepdims=True) / WIDTH
        total = total * lax.rsqrt(mean + norm_epsilon)
        gated, up = total[:, :128], total[:, 128:]
        acts[s, c, z] = (gated / (1.0 + jnp.exp(-gated)) * up).astype(BF)

        def send_act(k, carry):
            t, device = z_peer(k)
            remote(acts.at[s, c, z], acts.at[s, c, z], s_sem.at[18 + s], r_sem.at[18 + s], device).start()
            return carry

        lax.fori_loop(1, NZ, send_act, 0)

    def pair_acts(s):
        wait_bytes(acts.at[s, c, pl.ds(0, NZ - 1)], r_sem.at[18 + s])
        remote(acts.at[s, c], acts.at[s, c], s_sem.at[20 + s], r_sem.at[20 + s], sib).start()

    def down(s):
        wait_bytes(acts.at[s, 1 - c], r_sem.at[20 + s])
        act = jnp.concatenate(
            [acts[s, 0].reshape(tokens, 128), acts[s, 1].reshape(tokens, 128)], axis=1
        )
        down_s[s] = (dot_t(act, w_n[2]) * share[s]).astype(BF).reshape(NX, 128, LANES)
        down_r[s, x] = down_s[s, x]

        def send_down(k, carry):
            t = lax.rem(x + lax.rem(k, NX - 1) + 1, NX)
            part = pl.ds(pl.multiple_of(k // (NX - 1) * 64, 64), 64)
            remote(
                down_s.at[s, t, part], down_r.at[s, x, part], s_sem.at[22 + s],
                down_sem.at[s, k // (NX - 1)], {"ep": t * NY + y},
            ).start()
            return carry

        lax.fori_loop(0, 2 * (NX - 1), send_down, 0)

    def sum_x(s, half):
        part = pl.ds(64 * half, 64)
        wait_bytes(down_r.at[s, pl.ds(0, NX - 1), part], down_sem.at[s, half])
        total = down_r[s, 0, part].astype(F32)
        for k in range(1, NX):
            total = total + down_r[s, k, part].astype(F32)
        y_s[s, pl.ds(4 * half, 4)] = total.astype(BF).reshape(4, 16, LANES)
        for t in range(4 * half, 4 * half + 4):
            @pl.when(y == t)
            def _():
                y_r[s, t] = y_s[s, t]

            @pl.when(y != t)
            def _():
                remote(
                    y_s.at[s, t], y_r.at[s, y], s_sem.at[24 + s], r_sem.at[24 + s], {"ep": x * NY + t}
                ).start()

    def sum_y(s):
        wait_bytes(y_r.at[s, pl.ds(0, NY - 1)], r_sem.at[24 + s])
        routed = y_r[s, 0].astype(F32)
        for k in range(1, NY):
            routed = routed + y_r[s, k].astype(F32)
        fin_s[:, s, :] = hid[s] + routed

    heads_relay(0)
    heads_start(1)
    heads_relay(1)
    lax.fori_loop(1, NE, send_gates, 0)
    project(0)
    project_sum(0)
    project(1)
    project_sum(1)
    move(0)
    wait_bytes(res_r.at[pl.ds(0, NL - 1)], r_sem.at[0])
    rows_start(0)
    move(1)
    rows_relay(0)
    rows_start(1)
    arrange_gates()
    gate(0)
    rows_relay(1)
    lax.fori_loop(1, NE, send_downs, 0)
    pair_sum(0)
    gate(1)
    activate(0)
    pair_sum(1)
    arrange_downs()
    pair_acts(0)
    down(0)
    activate(1)
    sum_x(0, 0)
    sum_x(0, 1)
    pair_acts(1)
    down(1)
    sum_y(0)
    sum_x(1, 0)
    sum_x(1, 1)
    sum_y(1)

    def send_fin(k, carry):
        t = lax.rem(l + k, NL)
        remote(fin_s.at[t], fin_r.at[l], s_sem.at[26], r_sem.at[26], {"learn": t}).start()
        return carry

    lax.fori_loop(1, NL, send_fin, 0)
    fin_r[l] = fin_s[l]
    wait_bytes(fin_r.at[pl.ds(0, NL - 1)], r_sem.at[26])
    for k in range(NL):
        out_ref[:, SLICE * k : SLICE * k + SLICE] = fin_r[k][:, :SLICE]

    wait_bytes(res_r.at[pl.ds(0, NL - 1)], s_sem.at[0])
    wait_bytes(w_r.at[pl.ds(0, NE - 1), pl.ds(0, 32)], s_sem.at[3])
    wait_bytes(w_r.at[pl.ds(0, NE - 1), pl.ds(32, 16)], s_sem.at[29])
    wait_bytes(fin_r.at[pl.ds(0, NL - 1)], s_sem.at[26])
    for s in range(STEPS):
        wait_bytes(heads.at[s, pl.ds(0, NE - 1)], s_sem.at[1 + s])
        wait_bytes(att_r.at[s, pl.ds(0, NZ - 1)], s_sem.at[4 + s])
        wait_bytes(pair_s.at[s], s_sem.at[27 + s])
        move_wait(s, s_sem.at[6 + s])
        wait_bytes(rows.at[s, pl.ds(0, NE - 1)], s_sem.at[8 + s])
        wait_bytes(gate_s.at[s], s_sem.at[10 + s])
        wait_bytes(sq_s.at[s], s_sem.at[12 + s])
        wait_bytes(sum_s.at[s, pl.ds(0, NZ - 1)], s_sem.at[14 + s])
        wait_bytes(sq_z.at[s, pl.ds(0, NZ - 1)], s_sem.at[16 + s])
        wait_bytes(acts.at[s, 0, pl.ds(0, NZ - 1)], s_sem.at[18 + s])
        wait_bytes(acts.at[s, 0], s_sem.at[20 + s])
        wait_bytes(down_s.at[s, pl.ds(0, NX - 1)], s_sem.at[22 + s])
        wait_bytes(y_s.at[s, pl.ds(0, NY - 1)], s_sem.at[24 + s])


def layer(*operands):
    anywhere = pl.BlockSpec(memory_space=pl.ANY)
    vmem = pl.BlockSpec(memory_space=pltpu.VMEM)
    scratch = [pltpu.VMEM(a.shape, a.dtype) for a in operands] + [
        pltpu.VMEM((NE, 48, 256), BF),
        pltpu.VMEM((2, NE, 16, 256), BF),
        pltpu.VMEM((2, 256, PART), BF),
        pltpu.VMEM((2, 256, PART), BF),
        pltpu.VMEM((2, 256, PART), F32),
        pltpu.VMEM((2, NZ, 32, PART), BF),
        pltpu.VMEM((2, NZ, 32, PART), BF),
        pltpu.VMEM((2, 2, 16, PART), BF),
        pltpu.VMEM((2, 2, 16, PART), BF),
        pltpu.VMEM((NL, 2, LANES), F32),
        pltpu.VMEM((NL, 2, LANES), F32),
        pltpu.VMEM((2, 16, LANES), F32),
        pltpu.VMEM((2, NE, 16, LANES), BF),
        pltpu.VMEM((NE, 48, 256), BF),
        pltpu.VMEM((3, LANES, 256), BF),
        pltpu.VMEM((2, 512, 256), BF),
        pltpu.VMEM((2, 512, 256), F32),
        pltpu.VMEM((2, 512, 256), BF),
        pltpu.VMEM((2, NZ, 64, 256), BF),
        pltpu.VMEM((2, NZ, 64, 256), BF),
        pltpu.VMEM((2, 4, 1, 128), F32),
        pltpu.VMEM((2, 4, 1, 128), F32),
        pltpu.VMEM((2, 4, 1, 128), F32),
        pltpu.VMEM((2, NZ, 1, 128), F32),
        pltpu.VMEM((2, 2, NZ, 64, 128), BF),
        pltpu.VMEM((2, NX, 128, LANES), BF),
        pltpu.VMEM((2, NX, 128, LANES), BF),
        pltpu.VMEM((2, NY, 16, LANES), BF),
        pltpu.VMEM((2, NY, 16, LANES), BF),
        pltpu.VMEM((NL, 2, LANES), F32),
        pltpu.VMEM((NL, 2, LANES), F32),
        pltpu.VMEM((2, 512, 1), F32),
        pltpu.SemaphoreType.DMA((30,)),
        pltpu.SemaphoreType.DMA((30,)),
        pltpu.SemaphoreType.DMA((2, NY)),
        pltpu.SemaphoreType.DMA((2, NY)),
        pltpu.SemaphoreType.DMA((2, 2)),
        pltpu.SemaphoreType.DMA((15,)),
    ]
    return pl.pallas_call(
        layer_kernel,
        out_shape=jax.ShapeDtypeStruct((2, WIDTH), F32),
        in_specs=[anywhere] * len(operands),
        out_specs=vmem,
        scratch_shapes=scratch,
        compiler_params=pltpu.CompilerParams(
            collective_id=0, has_side_effects=True, vmem_limit_bytes=62 * 2**20
        ),
        name="decode_layer",
    )(*operands)


def per_device(
    master_weight, gradient, first_moment, second_moment, block_slot, queries, kv_cache, new_latent,
    lengths, uv_weight, out_weight, residual, norm_gain, expert_ids, route_weight,
):
    return layer(
        master_weight,
        gradient,
        first_moment,
        second_moment,
        block_slot.reshape(1, NE),
        queries,
        kv_cache.reshape(16 * CACHE, 576),
        new_latent.reshape(32, 576),
        lengths.reshape(1, 16),
        uv_weight,
        jnp.swapaxes(out_weight, 1, 2),
        residual.reshape(2, WIDTH),
        norm_gain.reshape(WIDTH // 128, 128),
        expert_ids,
        route_weight,
    ).reshape(2, 1, WIDTH).astype(BF)


def solution(mesh):
    in_specs = (
        P(("learn", "ep"), None, None, None),
        P(("learn", "ep"), None, None, None),
        P(("learn", "ep"), None, None, None),
        P(("learn", "ep"), None, None, None),
        P(),
        P(None, "ep", "learn", None),
        P("ep", None, None),
        P(None, "ep", None),
        P("ep"),
        P("learn", None, None),
        P("learn", None, "ep"),
        P(None, ("learn", "ep"), None),
        P(),
        P(None, ("learn", "ep"), None),
        P(None, ("learn", "ep"), None),
    )
    out_specs = P(None, ("learn", "ep"), None)
    return jax.shard_map(
        per_device, mesh=mesh, in_specs=in_specs, out_specs=out_specs, check_vma=False
    )
```

```python
import functools

import jax
import jax.numpy as jnp
from jax import lax
from jax.experimental import pallas as pl
from jax.experimental.pallas import tpu as pltpu
from jax.sharding import PartitionSpec as P

BF = jnp.bfloat16
F32 = jnp.float32
MESH = pl.DeviceIdType.MESH

beta_one = 0.9
beta_two = 0.95
learn_rate = 0.01
adam_step = 50
adam_epsilon = 1e-08
norm_epsilon = 1e-06
route_scale = 2.827

NX, NY, NZ, NL, NE = 4, 8, 8, 16, 32
WIDTH, SLICE, PART = 7168, 448, 224
LANES = 512
SS_LANE, SHARE_HI, SHARE_LO = 448, 456, 464
EXPERTS, STEPS, CACHE, LAT = 8, 2, 24, 512


def dot(a, b):
    return jnp.dot(a, b, preferred_element_type=F32)


def dot_t(a, b):
    return lax.dot_general(a, b, (((1,), (1,)), ((), ())), preferred_element_type=F32)


def iota(shape, dim):
    return lax.broadcasted_iota(jnp.int32, shape, dim)


def wait_bytes(ref, sem):
    pltpu.make_async_copy(ref, ref, sem).wait()


def remote(src, dst, ssem, rsem, device):
    return pltpu.make_async_remote_copy(
        src_ref=src, dst_ref=dst, send_sem=ssem, recv_sem=rsem, device_id=device, device_id_type=MESH
    )


def far_first(k):
    return jnp.where(lax.rem(k, 2) == 0, 4 - k // 2, 4 + (k - 1) // 2)


def column(row, size):
    count = row.shape[1]
    hit = lax.rem(iota((size, count), 0), count) == iota((size, count), 1)
    return jnp.sum(jnp.where(hit, row, jnp.zeros_like(row)), axis=1, keepdims=True)


def layer_kernel(
    mw_in, gr_in, fm_in, sm_in, slot_in, q_in, kv_in, new_in, len_in, uv_in, ow_in,
    residual_in, gain_in, ids_in, route_in, out_ref,
    mw, gr, fm, sm, slot_ref, q_ref, kv_ref, new_ref, len_ref, uv_ref, ow_ref,
    residual_ref, gain_ref, ids_ref, route_ref,
    w_s, heads, pair_s, pair_r, att_o, att_s, att_r, mov_s, mov_r, res_s, res_r, hid, rows, w_r, w_n,
    gate_s, gate_o, gate_r, sum_s, sum_r, sq_s, sq_r, sq_t, sq_z, acts, down_s, down_r,
    y_s, y_r, fin_s, fin_r, share,
    s_sem, r_sem, hy_sem, xy_sem, down_sem, l_sem,
):
    l = lax.axis_index("learn")
    e = lax.axis_index("ep")
    x, y = e // NY, lax.rem(e, NY)
    z, c = l // 2, lax.rem(l, 2)
    sib = {"learn": l + 1 - 2 * c}

    pairs = (
        (q_in, q_ref), (kv_in, kv_ref), (new_in, new_ref), (len_in, len_ref), (uv_in, uv_ref),
        (residual_in, residual_ref), (ids_in, ids_ref), (route_in, route_ref), (ow_in, ow_ref),
        (slot_in, slot_ref), (gain_in, gain_ref), (mw_in, mw), (gr_in, gr), (fm_in, fm), (sm_in, sm),
    )
    loads = [pltpu.make_async_copy(src, dst, l_sem.at[i]) for i, (src, dst) in enumerate(pairs)]
    for load in loads[:11]:
        load.start()

    barrier = pltpu.get_barrier_semaphore()

    def greet_ep(k, carry):
        pl.semaphore_signal(barrier, inc=1, device_id={"ep": lax.rem(e + k, NE)}, device_id_type=MESH)
        return carry

    def greet_learn(k, carry):
        pl.semaphore_signal(barrier, inc=1, device_id={"learn": lax.rem(l + k, NL)}, device_id_type=MESH)
        return carry

    lax.fori_loop(1, NE, greet_ep, 0)
    lax.fori_loop(1, NL, greet_learn, 0)
    own_move = e // 2 == l
    for j in range(2):
        @pl.when(jnp.logical_not(jnp.logical_and(own_move, lax.rem(e, 2) == j)))
        def _():
            pl.semaphore_signal(
                barrier, inc=1, device_id={"learn": e // 2, "ep": 2 * l + j}, device_id_type=MESH
            )

    for load in loads[:5]:
        load.wait()
    for load in loads[11:]:
        load.start()

    cached = 16 * CACHE
    scale = 192.0 ** (-0.5)
    parts = []
    for s in range(STEPS):
        wide = q_ref[s].astype(F32)
        for h in range(2):
            parts.append(wide[:, h, :].astype(BF))
    q = jnp.concatenate(parts, axis=0)
    old, new = kv_ref[...], new_ref[...]
    old_score, new_score = dot_t(q, old) * scale, dot_t(q, new) * scale
    row, col = iota((64, cached), 0), iota((64, cached), 1)
    first = lax.rem(row, 16) * CACHE
    live = jnp.logical_and(col >= first, col < first + column(len_ref[...], 64))
    old_score = jnp.where(live, old_score, -1e30)
    row, col = iota((64, 32), 0), iota((64, 32), 1)
    live = jnp.logical_and(lax.rem(row, 16) == lax.rem(col, 16), jnp.logical_or(col < 16, row >= 32))
    new_score = jnp.where(live, new_score, -1e30)
    top = jnp.maximum(
        jnp.max(old_score, axis=1, keepdims=True), jnp.max(new_score, axis=1, keepdims=True)
    )
    old_score, new_score = jnp.exp(old_score - top), jnp.exp(new_score - top)
    norm = jnp.sum(old_score, axis=1, keepdims=True) + jnp.sum(new_score, axis=1, keepdims=True)
    latent = dot((old_score / norm).astype(BF), old[:, :LAT])
    latent = (latent + dot((new_score / norm).astype(BF), new[:, :LAT])).astype(BF)
    for s in range(STEPS):
        for h in range(2):
            start = s * 32 + h * 16
            heads[s, e, :, 128 * h : 128 * h + 128] = dot(
                latent[start : start + 16], uv_ref[h]
            ).astype(BF)

    def gather_start(buf, i, ysem, xsem):
        def send_y(k, carry):
            t = x * NY + lax.rem(y + k, NY)
            remote(buf.at[e], buf.at[e], s_sem.at[i], ysem.at[k], {"ep": t}).start()
            return carry

        def send_x(k, carry):
            t = lax.rem(x + k, NX) * NY + y
            remote(buf.at[e], buf.at[e], s_sem.at[i], xsem, {"ep": t}).start()
            return carry

        lax.fori_loop(1, NY, send_y, 0)
        lax.fori_loop(1, NX, send_x, 0)

    def gather_relay(buf, i, ysem, xsem):
        def relay(t, carry):
            half = t // 2
            k = jnp.where(lax.rem(t, 2) == 0, half + 1, NY - 1 - half)
            o = x * NY + lax.rem(y + NY - k, NY)
            wait_bytes(buf.at[o], ysem.at[k])

            def send_x(j, carry2):
                d = lax.rem(x + j, NX) * NY + y
                remote(buf.at[o], buf.at[o], s_sem.at[i], xsem, {"ep": d}).start()
                return carry2

            return lax.fori_loop(1, NX, send_x, carry)

        lax.fori_loop(0, NY - 1, relay, 0)

    def heads_start(s):
        gather_start(heads.at[s], 1 + s, hy_sem.at[s], r_sem.at[1 + s])

    pl.semaphore_wait(barrier, NE - 1 + NL - 1 + 2 - own_move.astype(jnp.int32))
    heads_start(0)

    for load in loads[5:]:
        load.wait()
    lane8 = iota((8, LANES - SLICE), 1)
    hi_expert, lo_expert = lane8 - (SHARE_HI - SLICE), lane8 - (SHARE_LO - SLICE)
    tails = []
    for s in range(STEPS):
        ids = column(ids_ref[s], 8)
        weight = route_ref[s]
        route = column(weight / jnp.sum(weight, axis=1, keepdims=True) * route_scale, 8)
        hit = jnp.logical_or(
            jnp.logical_and(ids == hi_expert, hi_expert < EXPERTS),
            jnp.logical_and(ids == lo_expert, lo_expert < EXPERTS),
        )
        tails.append(jnp.sum(jnp.where(hit, route, 0.0), axis=0, keepdims=True))
    tail = jnp.concatenate(tails, axis=0)
    lines = residual_ref[...].astype(F32)
    for k in range(NL):
        res_s[k] = jnp.concatenate([lines[:, SLICE * k : SLICE * k + SLICE], tail], axis=1)
    res_r[l] = res_s[l]

    def send_res(k, carry):
        t = lax.rem(l + k, NL)
        remote(res_s.at[t], res_r.at[l], s_sem.at[0], r_sem.at[0], {"learn": t}).start()
        return carry

    lax.fori_loop(1, NL, send_res, 0)

    depth = mw.shape[0]
    count = depth * NE
    slots = column(slot_ref[...], NE).astype(F32)
    fits = lax.rem(iota((NE, count), 1), NE) == iota((NE, count), 0)
    slot_row = jnp.sum(jnp.where(fits, slots, 0.0), axis=0, keepdims=True).astype(jnp.int32)
    out_row, in_row = iota((NE * 16, count), 0), iota((NE * 16, count), 1)
    order = jnp.logical_and(out_row // 16 == slot_row, lax.rem(out_row, 16) == in_row // NE).astype(BF)
    first_scale = learn_rate / (1.0 - beta_one**adam_step)
    second_scale = 1.0 / (1.0 - beta_two**adam_step)
    for mat in range(3):
        g = gr[:, mat].astype(F32)
        first_new = beta_one * fm[:, mat].astype(F32) + (1.0 - beta_one) * g
        second_new = beta_two * sm[:, mat].astype(F32) + (1.0 - beta_two) * g * g
        stride = first_new * first_scale / (jnp.sqrt(second_new * second_scale) + adam_epsilon)
        updated = (mw[:, mat] - stride).astype(BF).reshape(count, 256)
        w_s[:, 16 * mat : 16 * mat + 16, :] = dot(order, updated).reshape(NE, 16, 256).astype(BF)

    w_r[e] = w_s[e]

    def send_gates(k, carry):
        t = lax.rem(e + k, NE)
        remote(
            w_s.at[t, pl.ds(0, 32)], w_r.at[e, pl.ds(0, 32)], s_sem.at[3], r_sem.at[3], {"ep": t}
        ).start()
        return carry

    def send_downs(k, carry):
        t = lax.rem(e + k, NE)
        remote(
            w_s.at[t, pl.ds(32, 16)], w_r.at[e, pl.ds(32, 16)], s_sem.at[29], r_sem.at[29], {"ep": t}
        ).start()
        return carry

    tokens = 512
    n, m = iota((tokens // 2, tokens), 0), iota((tokens // 2, tokens), 1)
    group = 4 * (n // 32) + lax.rem(n // 16, 2)
    picked = m - 32 * lax.rem(n, 16) - group
    reorder_own = (picked == 2 * c).astype(BF)
    reorder_sib = (picked == 2 - 2 * c).astype(BF)

    def z_peer(k):
        t = lax.rem(z + far_first(k), NZ)
        return t, {"learn": 2 * t + c}

    def heads_relay(s):
        gather_relay(heads.at[s], 1 + s, hy_sem.at[s], r_sem.at[1 + s])

    def project(s):
        wait_bytes(heads.at[s, pl.ds(0, NE - NY)], r_sem.at[1 + s])
        flat = heads[s].reshape(tokens, 256)

        def half(order):
            ordered = dot(order, flat).astype(BF)
            return dot_t(ordered[:, :128], ow_ref[0]) + dot_t(ordered[:, 128:], ow_ref[1])

        pair_s[s] = half(reorder_sib).astype(BF)
        remote(pair_s.at[s], pair_r.at[s], s_sem.at[27 + s], r_sem.at[27 + s], sib).start()
        att_o[s] = half(reorder_own)

    def project_sum(s):
        wait_bytes(pair_r.at[s], r_sem.at[27 + s])
        att_s[s] = (att_o[s] + pair_r[s].astype(F32)).astype(BF).reshape(NZ, 32, PART)
        att_r[s, z] = att_s[s, z]

        def send_att(k, carry):
            t, device = z_peer(k)
            remote(att_s.at[s, t], att_r.at[s, z], s_sem.at[4 + s], r_sem.at[4 + s], device).start()
            return carry

        lax.fori_loop(1, NZ, send_att, 0)

    def move(s):
        wait_bytes(att_r.at[s, pl.ds(0, NZ - 1)], r_sem.at[4 + s])
        total = att_r[s, 0].astype(F32)
        for k in range(1, NZ):
            total = total + att_r[s, k].astype(F32)
        mov_s[s] = total.astype(BF).reshape(2, 16, PART)
        for j in range(2):
            here = jnp.logical_and(own_move, lax.rem(e, 2) == j)

            @pl.when(here)
            def _():
                mov_r[s, lax.rem(e, 2)] = mov_s[s, j]

            @pl.when(jnp.logical_not(here))
            def _():
                remote(
                    mov_s.at[s, j], mov_r.at[s, lax.rem(e, 2)], s_sem.at[6 + s], r_sem.at[6 + s],
                    {"learn": e // 2, "ep": 2 * l + j},
                ).start()

    def move_wait(s, sem):
        @pl.when(own_move)
        def _():
            wait_bytes(mov_r.at[s, 0], sem)

        @pl.when(jnp.logical_not(own_move))
        def _():
            wait_bytes(mov_r.at[s], sem)

    gains = gain_ref[pl.ds(7 * z, 7), :]
    even = jnp.concatenate([gains[k : k + 1] for k in range(4)], axis=1)
    odd = jnp.concatenate([gains[k : k + 1] for k in range(3, 7)], axis=1)
    odd = jnp.concatenate([odd[:, 64:], odd[:, :64]], axis=1)
    gain = jnp.where(c == 0, even, odd)
    lane = iota((16, LANES), 1)
    spread_row, spread_col = iota((PART, LANES), 0), iota((PART, LANES), 1)
    place0 = (spread_col == spread_row).astype(BF)
    place1 = (spread_col == spread_row + PART).astype(BF)

    def rows_start(s):
        move_wait(s, r_sem.at[6 + s])
        attended = dot(mov_r[s, 0], place0) + dot(mov_r[s, 1], place1)
        value = res_r[:, s, :] + attended
        hid[s] = value
        squares = jnp.sum(jnp.where(lane < SLICE, value * value, 0.0), axis=1, keepdims=True)
        squares_hi = squares.astype(BF).astype(F32)
        value_hi = value.astype(BF).astype(F32)
        scaled = value * gain
        scaled = jnp.where(lane == SS_LANE, squares_hi, scaled)
        scaled = jnp.where(lane == SS_LANE + 1, squares - squares_hi, scaled)
        in_hi = jnp.logical_and(lane >= SHARE_HI, lane < SHARE_HI + EXPERTS)
        in_lo = jnp.logical_and(lane >= SHARE_LO, lane < SHARE_LO + EXPERTS)
        scaled = jnp.where(in_hi, value_hi, scaled)
        scaled = jnp.where(in_lo, value - value_hi, scaled)
        rows[s, e] = scaled.astype(BF)
        gather_start(rows.at[s], 8 + s, xy_sem.at[s], r_sem.at[8 + s])

    pn, pm = iota((LANES, LANES), 0), iota((LANES, LANES), 1)
    pick = jnp.logical_and(pn < SLICE, pm == pn + 2 * (pn // 14)).astype(BF)

    def natural(mat):
        return dot(pick, w_r[:, 16 * mat : 16 * mat + 16, :].reshape(LANES, 256)).astype(BF)

    def arrange_gates():
        wait_bytes(w_r.at[pl.ds(0, NE - 1), pl.ds(0, 32)], r_sem.at[3])
        for mat in range(2):
            block = natural(mat)
            for half in range(2):
                w_n[half, :, 128 * mat : 128 * mat + 128] = block[:, 128 * half : 128 * half + 128]

    def arrange_downs():
        wait_bytes(w_r.at[pl.ds(0, NE - 1), pl.ds(32, 16)], r_sem.at[29])
        w_n[2] = natural(2)

    ones_at = iota((16, LANES), 1)
    stat_row = jnp.logical_or(ones_at == SS_LANE, ones_at == SS_LANE + 1).astype(BF)
    tail_lane = iota((tokens, 128), 1) + 384
    mine = jnp.logical_or(tail_lane == SHARE_HI + e // 4, tail_lane == SHARE_LO + e // 4)

    def rows_relay(s):
        gather_relay(rows.at[s], 8 + s, xy_sem.at[s], r_sem.at[8 + s])

    def gate(s):
        wait_bytes(rows.at[s, pl.ds(0, NE - NY)], r_sem.at[8 + s])
        flat = rows[s].reshape(tokens, LANES)
        gate_s[s] = dot(flat, w_n[1 - c]).astype(BF)
        remote(gate_s.at[s], gate_r.at[s], s_sem.at[10 + s], r_sem.at[10 + s], sib).start()
        stat = dot_t(stat_row, flat)
        for t in range(4):
            sq_s[s, t] = stat[0:1, 128 * t : 128 * t + 128]
        remote(sq_s.at[s], sq_r.at[s], s_sem.at[12 + s], r_sem.at[12 + s], sib).start()
        gate_o[s] = dot(flat, w_n[c])
        share[s] = jnp.sum(jnp.where(mine, flat[:, 384:].astype(F32), 0.0), axis=1, keepdims=True)

    def pair_sum(s):
        wait_bytes(gate_r.at[s], r_sem.at[10 + s])
        wait_bytes(sq_r.at[s], r_sem.at[12 + s])
        sum_s[s] = (gate_o[s] + gate_r[s].astype(F32)).astype(BF).reshape(NZ, 64, 256)
        sq_t[s] = sq_s[s] + sq_r[s]
        sum_r[s, z] = sum_s[s, z]
        sq_z[s, z] = sq_t[s, z // 2]

        def send_sum(k, carry):
            t, device = z_peer(k)
            remote(sq_t.at[s, t // 2], sq_z.at[s, z], s_sem.at[16 + s], r_sem.at[16 + s], device).start()
            remote(sum_s.at[s, t], sum_r.at[s, z], s_sem.at[14 + s], r_sem.at[14 + s], device).start()
            return carry

        lax.fori_loop(1, NZ, send_sum, 0)

    sq_row, sq_lane = iota((64, 128), 0), iota((64, 128), 1)
    own_lane = sq_lane == sq_row + 64 * lax.rem(z, 2)

    def activate(s):
        wait_bytes(sum_r.at[s, pl.ds(0, NZ - 1)], r_sem.at[14 + s])
        wait_bytes(sq_z.at[s, pl.ds(0, NZ - 1)], r_sem.at[16 + s])
        total = sum_r[s, 0].astype(F32)
        squares = sq_z[s, 0]
        for k in range(1, NZ):
            total = total + sum_r[s, k].astype(F32)
            squares = squares + sq_z[s, k]
        mean = jnp.sum(jnp.where(own_lane, squares, 0.0), axis=1, keepdims=True) / WIDTH
        total = total * lax.rsqrt(mean + norm_epsilon)
        gated, up = total[:, :128], total[:, 128:]
        acts[s, c, z] = (gated / (1.0 + jnp.exp(-gated)) * up).astype(BF)

        def send_act(k, carry):
            t, device = z_peer(k)
            remote(acts.at[s, c, z], acts.at[s, c, z], s_sem.at[18 + s], r_sem.at[18 + s], device).start()
            return carry

        lax.fori_loop(1, NZ, send_act, 0)

    def pair_acts(s):
        wait_bytes(acts.at[s, c, pl.ds(0, NZ - 1)], r_sem.at[18 + s])
        remote(acts.at[s, c], acts.at[s, c], s_sem.at[20 + s], r_sem.at[20 + s], sib).start()

    def down(s):
        wait_bytes(acts.at[s, 1 - c], r_sem.at[20 + s])
        act = jnp.concatenate(
            [acts[s, 0].reshape(tokens, 128), acts[s, 1].reshape(tokens, 128)], axis=1
        )
        down_s[s] = (dot_t(act, w_n[2]) * share[s]).astype(BF).reshape(NX, 128, LANES)
        down_r[s, x] = down_s[s, x]

        def send_down(k, carry):
            t = lax.rem(x + lax.rem(k, NX - 1) + 1, NX)
            part = pl.ds(pl.multiple_of(k // (NX - 1) * 64, 64), 64)
            remote(
                down_s.at[s, t, part], down_r.at[s, x, part], s_sem.at[22 + s],
                down_sem.at[s, k // (NX - 1)], {"ep": t * NY + y},
            ).start()
            return carry

        lax.fori_loop(0, 2 * (NX - 1), send_down, 0)

    def sum_x(s, half):
        part = pl.ds(64 * half, 64)
        wait_bytes(down_r.at[s, pl.ds(0, NX - 1), part], down_sem.at[s, half])
        total = down_r[s, 0, part].astype(F32)
        for k in range(1, NX):
            total = total + down_r[s, k, part].astype(F32)
        y_s[s, pl.ds(4 * half, 4)] = total.astype(BF).reshape(4, 16, LANES)
        for t in range(4 * half, 4 * half + 4):
            @pl.when(y == t)
            def _():
                y_r[s, t] = y_s[s, t]

            @pl.when(y != t)
            def _():
                remote(
                    y_s.at[s, t], y_r.at[s, y], s_sem.at[24 + s], r_sem.at[24 + s], {"ep": x * NY + t}
                ).start()

    def sum_y(s):
        wait_bytes(y_r.at[s, pl.ds(0, NY - 1)], r_sem.at[24 + s])
        routed = y_r[s, 0].astype(F32)
        for k in range(1, NY):
            routed = routed + y_r[s, k].astype(F32)
        fin_s[:, s, :] = hid[s] + routed

    heads_relay(0)
    heads_start(1)
    heads_relay(1)
    lax.fori_loop(1, NE, send_gates, 0)
    project(0)
    project_sum(0)
    project(1)
    project_sum(1)
    move(0)
    wait_bytes(res_r.at[pl.ds(0, NL - 1)], r_sem.at[0])
    rows_start(0)
    move(1)
    rows_relay(0)
    rows_start(1)
    arrange_gates()
    gate(0)
    rows_relay(1)
    lax.fori_loop(1, NE, send_downs, 0)
    pair_sum(0)
    gate(1)
    activate(0)
    pair_sum(1)
    arrange_downs()
    pair_acts(0)
    down(0)
    activate(1)
    sum_x(0, 0)
    sum_x(0, 1)
    pair_acts(1)
    down(1)
    sum_y(0)
    sum_x(1, 0)
    sum_x(1, 1)
    sum_y(1)

    def send_fin(k, carry):
        t = lax.rem(l + k, NL)
        remote(fin_s.at[t], fin_r.at[l], s_sem.at[26], r_sem.at[26], {"learn": t}).start()
        return carry

    lax.fori_loop(1, NL, send_fin, 0)
    fin_r[l] = fin_s[l]
    wait_bytes(fin_r.at[pl.ds(0, NL - 1)], r_sem.at[26])
    for k in range(NL):
        out_ref[:, SLICE * k : SLICE * k + SLICE] = fin_r[k][:, :SLICE]

    wait_bytes(res_r.at[pl.ds(0, NL - 1)], s_sem.at[0])
    wait_bytes(w_r.at[pl.ds(0, NE - 1), pl.ds(0, 32)], s_sem.at[3])
    wait_bytes(w_r.at[pl.ds(0, NE - 1), pl.ds(32, 16)], s_sem.at[29])
    wait_bytes(fin_r.at[pl.ds(0, NL - 1)], s_sem.at[26])
    for s in range(STEPS):
        wait_bytes(heads.at[s, pl.ds(0, NE - 1)], s_sem.at[1 + s])
        wait_bytes(att_r.at[s, pl.ds(0, NZ - 1)], s_sem.at[4 + s])
        wait_bytes(pair_s.at[s], s_sem.at[27 + s])
        move_wait(s, s_sem.at[6 + s])
        wait_bytes(rows.at[s, pl.ds(0, NE - 1)], s_sem.at[8 + s])
        wait_bytes(gate_s.at[s], s_sem.at[10 + s])
        wait_bytes(sq_s.at[s], s_sem.at[12 + s])
        wait_bytes(sum_s.at[s, pl.ds(0, NZ - 1)], s_sem.at[14 + s])
        wait_bytes(sq_z.at[s, pl.ds(0, NZ - 1)], s_sem.at[16 + s])
        wait_bytes(acts.at[s, 0, pl.ds(0, NZ - 1)], s_sem.at[18 + s])
        wait_bytes(acts.at[s, 0], s_sem.at[20 + s])
        wait_bytes(down_s.at[s, pl.ds(0, NX - 1)], s_sem.at[22 + s])
        wait_bytes(y_s.at[s, pl.ds(0, NY - 1)], s_sem.at[24 + s])


def layer(*operands):
    anywhere = pl.BlockSpec(memory_space=pl.ANY)
    vmem = pl.BlockSpec(memory_space=pltpu.VMEM)
    scratch = [pltpu.VMEM(a.shape, a.dtype) for a in operands] + [
        pltpu.VMEM((NE, 48, 256), BF),
        pltpu.VMEM((2, NE, 16, 256), BF),
        pltpu.VMEM((2, 256, PART), BF),
        pltpu.VMEM((2, 256, PART), BF),
        pltpu.VMEM((2, 256, PART), F32),
        pltpu.VMEM((2, NZ, 32, PART), BF),
        pltpu.VMEM((2, NZ, 32, PART), BF),
        pltpu.VMEM((2, 2, 16, PART), BF),
        pltpu.VMEM((2, 2, 16, PART), BF),
        pltpu.VMEM((NL, 2, LANES), F32),
        pltpu.VMEM((NL, 2, LANES), F32),
        pltpu.VMEM((2, 16, LANES), F32),
        pltpu.VMEM((2, NE, 16, LANES), BF),
        pltpu.VMEM((NE, 48, 256), BF),
        pltpu.VMEM((3, LANES, 256), BF),
        pltpu.VMEM((2, 512, 256), BF),
        pltpu.VMEM((2, 512, 256), F32),
        pltpu.VMEM((2, 512, 256), BF),
        pltpu.VMEM((2, NZ, 64, 256), BF),
        pltpu.VMEM((2, NZ, 64, 256), BF),
        pltpu.VMEM((2, 4, 1, 128), F32),
        pltpu.VMEM((2, 4, 1, 128), F32),
        pltpu.VMEM((2, 4, 1, 128), F32),
        pltpu.VMEM((2, NZ, 1, 128), F32),
        pltpu.VMEM((2, 2, NZ, 64, 128), BF),
        pltpu.VMEM((2, NX, 128, LANES), BF),
        pltpu.VMEM((2, NX, 128, LANES), BF),
        pltpu.VMEM((2, NY, 16, LANES), BF),
        pltpu.VMEM((2, NY, 16, LANES), BF),
        pltpu.VMEM((NL, 2, LANES), F32),
        pltpu.VMEM((NL, 2, LANES), F32),
        pltpu.VMEM((2, 512, 1), F32),
        pltpu.SemaphoreType.DMA((30,)),
        pltpu.SemaphoreType.DMA((30,)),
        pltpu.SemaphoreType.DMA((2, NY)),
        pltpu.SemaphoreType.DMA((2, NY)),
        pltpu.SemaphoreType.DMA((2, 2)),
        pltpu.SemaphoreType.DMA((15,)),
    ]
    return pl.pallas_call(
        layer_kernel,
        out_shape=jax.ShapeDtypeStruct((2, WIDTH), F32),
        in_specs=[anywhere] * len(operands),
        out_specs=vmem,
        scratch_shapes=scratch,
        compiler_params=pltpu.CompilerParams(
            collective_id=0, has_side_effects=True, vmem_limit_bytes=62 * 2**20
        ),
        name="decode_layer",
    )(*operands)


def per_device(
    master_weight, gradient, first_moment, second_moment, block_slot, queries, kv_cache, new_latent,
    lengths, uv_weight, out_weight, residual, norm_gain, expert_ids, route_weight,
):
    return layer(
        master_weight,
        gradient,
        first_moment,
        second_moment,
        block_slot.reshape(1, NE),
        queries,
        kv_cache.reshape(16 * CACHE, 576),
        new_latent.reshape(32, 576),
        lengths.reshape(1, 16),
        uv_weight,
        jnp.swapaxes(out_weight, 1, 2),
        residual.reshape(2, WIDTH),
        norm_gain.reshape(WIDTH // 128, 128),
        expert_ids,
        route_weight,
    ).reshape(2, 1, WIDTH).astype(BF)


def solution(mesh):
    in_specs = (
        P(("learn", "ep"), None, None, None),
        P(("learn", "ep"), None, None, None),
        P(("learn", "ep"), None, None, None),
        P(("learn", "ep"), None, None, None),
        P(),
        P(None, "ep", "learn", None),
        P("ep", None, None),
        P(None, "ep", None),
        P("ep"),
        P("learn", None, None),
        P("learn", None, "ep"),
        P(None, ("learn", "ep"), None),
        P(),
        P(None, ("learn", "ep"), None),
        P(None, ("learn", "ep"), None),
    )
    out_specs = P(None, ("learn", "ep"), None)
    return jax.shard_map(
        per_device, mesh=mesh, in_specs=in_specs, out_specs=out_specs, check_vma=False
    )
```
